256 devices in a mesh: section: 16 (over y_hi, z), expert: 16 (over x, y_lo, core).
Axes of the slice: x: 4, y: 4 (y_hi: 2, y_lo: 2; y = y_hi * 2 + y_lo), z: 8, core: 2. Of those that a mesh axis runs over, the one named last changes fastest.
Arguments:
- tokens: bfloat16 [16, 2048, 3584], P('section', 'expert'), may hold values from -6 to 6
- norm_gain: float32 [16, 3584], P('section'), may hold values from 0.1 to 1.9
- expert_ids: int32 [16, 2048, 2], P('section', 'expert'), may hold values from 0 to 3, all different within a row; in each aligned block of 128 rows (0 to 127, 128 to 255, ..., all dimensions but the last counted through in order) at most 80 rows name the same one
- gate_values: float32 [16, 2048, 2], P('section', 'expert'), may hold values from 0.2 to 1
- gate_weight: bfloat16 [16, 3584, 8192], P('section', None, 'expert'), may hold values from -0.09375 to 0.09375
- up_weight: bfloat16 [16, 3584, 8192], P('section', None, 'expert'), may hold values from -0.09375 to 0.09375
- down_weight: bfloat16 [16, 8192, 3584], P('section', 'expert'), may hold values from -0.125 to 0.125
Outputs:
- handed: bfloat16 [16, 2048, 3584], P('section', 'expert')
The draws below stay inside these ranges and needn't reach their ends.
Inputs may be any that keep to these rules, and one draw needn't show every extreme that they name: `expert_ids`: each token names 2 different experts. Of the 128 tokens of one device (aligned blocks of 128 rows), at most 80 choose any one expert, and exactly 80 choose some expert in some blocks.
All inputs are finite; a program needn't handle non-finite values.
Results may differ from the reference program's by a relative error of at most 0.0053.
Values may be sent and summed in bfloat16 or wider, within the bound.
No kernel may reach another device: no remote copies, remote signals or barrier semaphores. Data moves between devices by JAX's collectives and lax.ppermute only.
A program may use at most 128 MiB of HBM per device.

```python
import math
import jax
import jax.numpy as jnp
import numpy as np
from jax import lax

D = 3584
FF = 2048
EXPERTS = 4
TOP = 2
TOK_DEV = 128
CAP = 80
MB = 2048
N_SECTION = 16
N_EXPERT = 16


def steps_of(rng, extent, split, least, high):
    def one(position, blocks):
        steps = jax.random.uniform(jax.random.fold_in(jax.random.fold_in(rng, 6), position), (blocks,), jnp.float32, least / len(split), high / len(split))
        return jnp.repeat(jnp.exp(steps), extent[position] // blocks).reshape((-1,) + (1,) * (len(extent) - position - 1))

    level = one(*split[0])
    for cut in split[1:]:
        level = level * one(*cut)
    return level


def shared_out(key, own, number, rows, count, top, bound, slope):
    sequence = jax.random.permutation(key, count)
    heavy_load, ordinary = shares(count, rows * top, bound, slope, True), shares(count, rows * top, bound, slope, False)
    places = jnp.arange(count)

    def named(tallies, rotation):
        used = int((tallies > 0).sum())
        fixed = max(1, used // 4)
        shifted = fixed + (places - fixed + rotation * (used - fixed)) % max(1, count - fixed)
        return jnp.zeros((count,), jnp.int32).at[sequence[jnp.where(places < fixed, places, shifted)]].set(jnp.asarray(tallies, jnp.int32))

    tallies = jnp.where(number % 4 == 0, named(heavy_load, number // 4), named(ordinary, number - number // 4 - 1))
    mixed = jax.random.permutation(jax.random.fold_in(own, 3), count)
    source_of, receiver = mixed[0:count // 2 * 2:2], mixed[1:count // 2 * 2:2]
    room = jnp.minimum(tallies[source_of] - 1, bound - tallies[receiver]) // 2
    room = jnp.where((source_of == sequence[0]) | (receiver == sequence[0]) | (tallies[receiver] == 0), 0, jnp.maximum(room, 0))
    shifted = jax.random.randint(jax.random.fold_in(own, 4), (count // 2,), 0, 1 << 20) % (room + 1)
    tallies = tallies.at[source_of].add(-shifted).at[receiver].add(shifted)
    items = jnp.searchsorted(jnp.cumsum(tallies), jnp.arange(rows * top), side="right").astype(jnp.int32)
    grid = items.reshape(top, rows).T
    grid = grid[jax.random.permutation(jax.random.fold_in(own, 1), rows)]
    rotation = jax.random.randint(jax.random.fold_in(own, 2), (rows, 1), 0, top)
    return jnp.take_along_axis(grid, (jnp.arange(top)[None, :] + rotation) % top, axis=1)


def shares(number_of, total, most, skew, full):
    weights = [(1 << 20) // math.isqrt(grade ** skew) + 1 for grade in range(1, number_of + 1)]
    largest = most if full else min(most, max(-(-total // number_of), total * weights[0] // sum(weights)))
    least = 1 if total - largest >= number_of - 1 else 0
    given, spare = [largest] + [least] * (number_of - 1), total - largest - least * (number_of - 1)
    while spare > 0:
        movable = [i for i in range(1, number_of) if given[i] < largest] or [i for i in range(1, number_of) if given[i] < most]
        mass, remaining = sum([weights[i] for i in movable]), spare
        for i in movable:
            addition = min(most - given[i], max(1, remaining * weights[i] // mass), spare)
            given[i] = given[i] + addition
            spare = spare - addition
    return np.array(given)


def normal_values(own_key, shape, scale, bound, split=(), kind=jnp.bfloat16):
    drawn = jax.random.normal(own_key, shape, jnp.float32) * scale
    if len(split) > 0:
        drawn = steps_of(own_key, shape, split, -0.22, 0.18) * drawn
    return jnp.clip(drawn, min=-bound, max=bound).astype(kind)


def setup_inputs(seed: int = 0) -> dict:
    key_of = jax.random.split(jax.random.key(seed), 8)
    tokens = normal_values(key_of[0], (N_SECTION, MB, D), 1.0, 6.0, ((0, 16), (1, 16)))
    norm_gain = jnp.clip(1.0 + 0.18 * jax.random.normal(key_of[1], (N_SECTION, D), jnp.float32), 0.1, 1.9)
    expert_ids_keys = jax.random.split(jax.random.fold_in(key_of[2], 1), N_SECTION * MB // TOK_DEV)
    expert_ids_turns = jax.random.permutation(jax.random.fold_in(key_of[2], 3), N_SECTION * MB // TOK_DEV)
    expert_ids = jax.vmap(lambda own, number: shared_out(jax.random.fold_in(key_of[2], 2), own, number, TOK_DEV, EXPERTS, TOP, CAP, 2))(expert_ids_keys, expert_ids_turns).reshape((N_SECTION, MB, TOP))
    gate_values = jnp.clip(0.2 + 0.8 * jax.random.uniform(key_of[3], (N_SECTION, MB, TOP), jnp.float32) ** steps_of(key_of[3], (N_SECTION, MB, TOP), ((0, 16), (1, 16)), -0.2, 0.2), 0.2, 1.0)
    gate_weight = normal_values(key_of[4], (N_SECTION, D, EXPERTS * FF), D ** -0.5, 0.09375, ((0, 16), (2, 16)))
    up_weight = normal_values(key_of[5], (N_SECTION, D, EXPERTS * FF), D ** -0.5, 0.09375, ((0, 16), (2, 16)))
    down_weight = normal_values(key_of[6], (N_SECTION, EXPERTS * FF, D), FF ** -0.5, 0.125, ((0, 16), (1, 16)))
    return {"tokens": tokens, "norm_gain": norm_gain, "expert_ids": expert_ids, "gate_values": gate_values, "gate_weight": gate_weight, "up_weight": up_weight, "down_weight": down_weight}


def expert_layer(resident, norm_gain, expert_ids, gate_values, gate_weight, up_weight, down_weight):
    shards = N_EXPERT // EXPERTS
    units = FF // shards
    limit = N_EXPERT * CAP
    widened = resident.astype(jnp.float32)
    scale = lax.rsqrt(lax.optimization_barrier(jnp.mean(widened * widened, axis=-1, keepdims=True)) + 1e-06)
    normed = (widened * scale * norm_gain.astype(jnp.float32)).astype(jnp.bfloat16)
    mixture = jnp.zeros(widened.shape, jnp.float32)
    for expert in range(EXPERTS):
        matches = expert_ids == expert
        chosen = jnp.any(matches, axis=-1)
        weight = lax.optimization_barrier(jnp.sum(jnp.where(matches, gate_values, jnp.zeros_like(gate_values)), axis=-1))
        picking = jnp.argsort(1 - chosen.astype(jnp.int32), stable=True)[:limit]
        routed = normed[picking]
        first = expert * FF
        gate = jnp.dot(routed, gate_weight[:, first:first + FF], preferred_element_type=jnp.float32)
        upward = jnp.dot(routed, up_weight[:, first:first + FF], preferred_element_type=jnp.float32)
        hidden = (jax.nn.silu(gate) * upward).astype(jnp.bfloat16)
        pieces = jnp.einsum('rsu,sud->rsd', hidden.astype(jnp.float32).reshape(limit, shards, units), down_weight[first:first + FF].astype(jnp.float32).reshape(shards, units, D))
        rounded = lax.optimization_barrier(pieces.astype(jnp.bfloat16)).astype(jnp.float32)
        summed = lax.optimization_barrier(jnp.sum(rounded, axis=1))
        mixture = mixture.at[picking].add(weight[picking][:, None] * summed)
    return (widened + mixture).astype(jnp.bfloat16)

def reference(tokens, norm_gain, expert_ids, gate_values, gate_weight, up_weight, down_weight):

    def one_section(parts):
        return expert_layer(*parts)
    outputs = lax.map(one_section, (tokens, norm_gain, expert_ids, gate_values, gate_weight, up_weight, down_weight))
    return jnp.roll(outputs, 1, axis=0)
```

```python
import functools

import jax
import jax.numpy as jnp
from jax import lax
from jax.experimental import pallas as pl
from jax.experimental.pallas import tpu as pltpu
from jax.sharding import PartitionSpec as P

EXPERTS = 4
CAP = 80
CHUNKS = 2
F32 = jnp.float32
BF16 = jnp.bfloat16


def moved(value, dx, dy, dc):
    pairs = []
    for i in range(16):
        x, y, c = i // 4, (i // 2) % 2, i % 2
        pairs.append((i, ((x + dx) % 4) * 4 + ((y + dy) % 2) * 2 + (c + dc) % 2))
    return lax.ppermute(value, "expert", pairs)


def shifted(shard, axis, by):
    devices = lax.axis_size(axis)
    return lax.ppermute(shard, axis, [(i, (i + by) % devices) for i in range(devices)])


def route_kernel(tok_ref, gain_ref, ids_ref, gv_ref, out_ref, high_ref, low_ref):
    wide = tok_ref[...].astype(F32)
    scale = lax.rsqrt(jnp.mean(wide * wide, axis=-1, keepdims=True) + 1e-06)
    normed = (wide * scale * gain_ref[...]).astype(BF16)
    count = wide.shape[0]
    first, second = ids_ref[0:1, :], ids_ref[1:2, :]
    kind = lax.broadcasted_iota(jnp.int32, (16, count), 0)
    chosen = (kind == first) | (kind == second)
    before = (
        lax.broadcasted_iota(jnp.int32, (count, count), 0)
        < lax.broadcasted_iota(jnp.int32, (count, count), 1)
    )
    place = jnp.dot(
        chosen.astype(F32).astype(BF16), before.astype(F32).astype(BF16), preferred_element_type=F32
    )
    weight = jnp.where(kind == first, gv_ref[0:1, :], 0.0) + jnp.where(
        kind == second, gv_ref[1:2, :], 0.0
    )
    slot = lax.broadcasted_iota(jnp.int32, (CAP, count), 0).astype(F32)
    for d in range(EXPERTS):
        spot = jnp.where(chosen[d : d + 1, :], place[d : d + 1, :], -1.0)
        hit = slot == spot
        pick = jnp.where(hit, 1.0, 0.0).astype(BF16)
        out_ref[d] = jnp.dot(pick, normed, preferred_element_type=F32).astype(BF16)
        full = jnp.where(hit, weight[d : d + 1, :], 0.0)
        high = full.astype(BF16)
        high_ref[d] = high
        low_ref[d] = (full - high.astype(F32)).astype(BF16)


def route(tok, gain, ids, gv):
    count, dim = tok.shape
    return pl.pallas_call(
        route_kernel,
        out_shape=(
            jax.ShapeDtypeStruct((EXPERTS, CAP, dim), BF16),
            jax.ShapeDtypeStruct((EXPERTS, CAP, count), BF16),
            jax.ShapeDtypeStruct((EXPERTS, CAP, count), BF16),
        ),
        in_specs=[pl.BlockSpec(memory_space=pltpu.VMEM)] * 4,
        out_specs=[pl.BlockSpec(memory_space=pltpu.VMEM)] * 3,
        cost_estimate=pl.CostEstimate(
            flops=2 * EXPERTS * CAP * count * dim, bytes_accessed=6 * count * dim, transcendentals=0
        ),
        compiler_params=pltpu.CompilerParams(vmem_limit_bytes=32 << 20),
        name="route",
    )(tok, gain, ids, gv)


def weighted(high, low, rows):
    dims = (((0,), (0,)), ((), ()))
    return lax.dot_general(high, rows, dims, preferred_element_type=F32) + lax.dot_general(
        low, rows, dims, preferred_element_type=F32
    )


def mix_kernel(kinds, extra, high_ref, low_ref, *refs):
    out_ref = refs[-1]
    total = None
    for kind, ref in zip(kinds, refs):
        part = weighted(high_ref[kind], low_ref[kind], ref[...])
        total = part if total is None else total + part
    for ref in refs[len(kinds) : len(kinds) + extra]:
        total = total + ref[...].astype(F32)
    out_ref[...] = total.astype(BF16)


def mix(kinds, high, low, blocks, extra):
    count, dim = high.shape[2], blocks[0].shape[1]
    tile = 896 if dim % 896 == 0 else dim
    return pl.pallas_call(
        functools.partial(mix_kernel, kinds, len(extra)),
        grid=(dim // tile,),
        out_shape=jax.ShapeDtypeStruct((count, dim), BF16),
        in_specs=[pl.BlockSpec((EXPERTS, CAP, count), lambda i: (0, 0, 0))] * 2
        + [pl.BlockSpec((CAP, tile), lambda i: (0, i))] * len(blocks)
        + [pl.BlockSpec((count, tile), lambda i: (0, i))] * len(extra),
        out_specs=pl.BlockSpec((count, tile), lambda i: (0, i)),
        cost_estimate=pl.CostEstimate(
            flops=4 * len(blocks) * CAP * count * dim,
            bytes_accessed=2 * dim * (len(blocks) * CAP + (len(extra) + 1) * count),
            transcendentals=0,
        ),
        name="mix",
    )(high, low, *blocks, *extra)


def on_device(tokens, norm_gain, expert_ids, gate_values, gate_weight, up_weight, down_weight):
    tok = tokens[0]
    dim = tok.shape[1]
    column = lax.axis_index("expert") // 4
    ids = (expert_ids[0].T - column + EXPERTS) % EXPERTS
    gv = gate_values[0].T
    tok_across = moved(tok, 0, 1, 0)
    choice = jnp.concatenate([ids.astype(F32), gv], axis=0)
    choice_across = moved(choice, 0, 1, 0)
    gates = (gate_weight[0], moved(gate_weight[0], 0, 0, 1))
    ups = (up_weight[0], moved(up_weight[0], 0, 0, 1))
    downs = (down_weight[0], moved(down_weight[0], 0, 0, 1))

    own, own_high, own_low = route(tok, norm_gain, ids, gv)
    own_far = moved(own[2], 2, 0, 0)
    own_right = moved(own[1], 1, 0, 0)
    own_left = moved(own[3], -1, 0, 0)
    across, across_high, across_low = route(
        tok_across, norm_gain, choice_across[:2].astype(jnp.int32), choice_across[2:]
    )
    across_right = moved(across[1], 1, 0, 0)
    across_left = moved(across[3], -1, 0, 0)
    across_far = moved(own_far, 0, 1, 0)

    def hidden_of(rows):
        result = []
        for gate_w, up_w in zip(gates, ups):
            gate = jnp.dot(rows, gate_w, preferred_element_type=F32)
            upward = jnp.dot(rows, up_w, preferred_element_type=F32)
            result.append((jax.nn.silu(gate) * upward).astype(BF16))
        return result

    def down_of(hidden, lo, hi):
        return (
            jnp.dot(hidden[0], downs[0][:, lo:hi], preferred_element_type=F32)
            + jnp.dot(hidden[1], downs[1][:, lo:hi], preferred_element_type=F32)
        ).astype(BF16)

    early = hidden_of(jnp.concatenate([own[0], across[0], own_far, own_right, own_left], axis=0))
    late = hidden_of(jnp.concatenate([across_far, across_right, across_left], axis=0))
    width = dim // CHUNKS
    outs = []
    for k in range(CHUNKS):
        lo, hi = k * width, (k + 1) * width
        late_out = down_of(late, lo, hi)
        early_out = down_of(early, lo, hi)
        blocks = [early_out[i * CAP : (i + 1) * CAP] for i in range(5)]
        late_blocks = [late_out[i * CAP : (i + 1) * CAP] for i in range(3)]
        far_in = moved(late_blocks[0], 0, 1, 0)
        back_right = moved(late_blocks[1], -1, 0, 0)
        back_left = moved(late_blocks[2], 1, 0, 0)
        my_right = moved(blocks[3], -1, 0, 0)
        my_left = moved(blocks[4], 1, 0, 0)
        far_sum = (blocks[2].astype(F32) + far_in.astype(F32)).astype(BF16)
        my_far = moved(far_sum, 2, 0, 0)
        theirs = mix((0, 1, 3), across_high, across_low, (blocks[1], back_right, back_left), ())
        mine = moved(theirs, 0, 1, 0)
        layer_out = mix(
            (0, 1, 3, 2),
            own_high,
            own_low,
            (blocks[0], my_right, my_left, my_far),
            (mine, tok[:, lo:hi]),
        )
        outs.append(shifted(layer_out, "section", 1))
    return jnp.concatenate(outs, axis=1)[None]


def solution(mesh):
    in_specs = (
        P("section", "expert", None),
        P("section", None),
        P("section", "expert", None),
        P("section", "expert", None),
        P("section", None, "expert"),
        P("section", None, "expert"),
        P("section", "expert", None),
    )
    out_specs = P("section", "expert", None)
    return jax.shard_map(
        on_device, mesh=mesh, in_specs=in_specs, out_specs=out_specs, check_vma=False
    )
```

```python
import functools

import jax
import jax.numpy as jnp
from jax import lax
from jax.experimental import pallas as pl
from jax.experimental.pallas import tpu as pltpu
from jax.sharding import PartitionSpec as P

EXPERTS = 4
CAP = 80
CHUNKS = 2
LAYERS = 8
TILE = 256
PACK = 128
FREE = pl.CostEstimate(flops=0, bytes_accessed=0, transcendentals=0)
F32 = jnp.float32
BF16 = jnp.bfloat16
VMEM = pl.BlockSpec(memory_space=pltpu.VMEM)
SMEM = pl.BlockSpec(memory_space=pltpu.SMEM)
ANY = pl.BlockSpec(memory_space=pl.ANY)
HBM = pl.BlockSpec(memory_space=pltpu.HBM)


def limit(mebibytes):
    return pltpu.CompilerParams(vmem_limit_bytes=mebibytes << 20)


def moved(value, dx, dy, dc):
    pairs = []
    for i in range(16):
        x, y, c = i // 4, (i // 2) % 2, i % 2
        pairs.append((i, ((x + dx) % 4) * 4 + ((y + dy) % 2) * 2 + (c + dc) % 2))
    return lax.ppermute(value, "expert", pairs)


def handed_on(value):
    pairs = []
    for s in range(16):
        for e in range(16):
            to = e ^ 2 if s % LAYERS == LAYERS - 1 else e
            pairs.append((s * 16 + e, ((s + 1) % 16) * 16 + to))
    return lax.ppermute(value, ("section", "expert"), pairs)


def first_route_kernel(column_ref, *refs):
    far, refs = refs[:4], refs[4:]
    *refs, sent_ref, gain_ref, ids_ref, gv_ref, sems = refs
    count, dim = far[0].shape
    near = (sent_ref.at[:, :dim], gain_ref, ids_ref, gv_ref)
    copies = [pltpu.make_async_copy(a, b, sems.at[i]) for i, (a, b) in enumerate(zip(far, near))]
    for copy in copies:
        copy.start()
    for copy in copies:
        copy.wait()
    ids, gv = ids_ref[...], gv_ref[...]
    high = gv.astype(BF16).astype(F32)
    middle = (gv - high).astype(BF16).astype(F32)
    low = gv - high - middle
    packed = jnp.concatenate([ids.astype(F32), high, middle, low], axis=0)
    packed = jnp.concatenate([packed, jnp.zeros((PACK - 8, count), F32)], axis=0)
    sent_ref[:, dim:] = packed.T.astype(BF16)
    route_kernel((0, 1, 2, 3), column_ref, sent_ref, gain_ref, ids, gv, *refs)


def second_route_kernel(column_ref, sent_ref, gain_ref, *refs):
    packed = sent_ref[:, gain_ref.shape[1] :].astype(F32).T
    ids = packed[0:2].astype(jnp.int32)
    gv = packed[2:4] + packed[4:6] + packed[6:8]
    route_kernel((0, 1, 3), column_ref, sent_ref, gain_ref, ids, gv, *refs)


def route_kernel(kinds, column_ref, tok_ref, gain_ref, ids, gv, *refs):
    w_ref = refs[-1]
    out_refs = dict(zip(kinds, refs[-1 - len(kinds) : -1]))
    wide = tok_ref[:, : gain_ref.shape[1]].astype(F32)
    scale = lax.rsqrt(jnp.mean(wide * wide, axis=-1, keepdims=True) + 1e-06)
    normed = (wide * scale * gain_ref[...]).astype(BF16)
    count = normed.shape[0]
    ids = jnp.bitwise_and(ids + (EXPERTS - column_ref[0]), EXPERTS - 1)
    first, second = ids[0:1, :], ids[1:2, :]
    kind = lax.broadcasted_iota(jnp.int32, (16, count), 0)
    chosen = (kind == first) | (kind == second)
    before = (
        lax.broadcasted_iota(jnp.int32, (count, count), 0)
        < lax.broadcasted_iota(jnp.int32, (count, count), 1)
    )
    place = jnp.dot(
        chosen.astype(F32).astype(BF16), before.astype(F32).astype(BF16), preferred_element_type=F32
    )
    weight = jnp.where(kind == first, gv[0:1, :], 0.0) + jnp.where(
        kind == second, gv[1:2, :], 0.0
    )
    slot = lax.broadcasted_iota(jnp.int32, (CAP, count), 0).astype(F32)
    for d in range(EXPERTS):
        spot = jnp.where(chosen[d : d + 1, :], place[d : d + 1, :], -1.0)
        hit = slot == spot
        pick = jnp.where(hit, 1.0, 0.0).astype(BF16)
        if d in out_refs:
            out_refs[d][...] = jnp.dot(pick, normed, preferred_element_type=F32).astype(BF16)
        full = jnp.where(hit, weight[d : d + 1, :], 0.0)
        high = full.astype(BF16)
        low = (full - high.astype(F32)).astype(BF16)
        w_ref[d] = jnp.concatenate([high, low], axis=1)


def route(first_set, column, tok, gain, choices, others):
    count, dim = tok.shape[0], gain.shape[1]
    blocks = 4 if first_set else 3
    out_shape = [jax.ShapeDtypeStruct((CAP, dim), BF16)] * blocks
    out_shape.append(jax.ShapeDtypeStruct((EXPERTS, CAP, 2 * count), BF16))
    kernel, scratch = second_route_kernel, []
    if first_set:
        kernel = first_route_kernel
        out_shape.append(jax.ShapeDtypeStruct((count, dim + PACK), BF16))
        scratch = [pltpu.VMEM(v.shape, v.dtype) for v in (gain, *choices)]
        scratch.append(pltpu.SemaphoreType.DMA((4,)))
    operands = (tok, gain, *choices)
    inner = 1 + len(operands)

    def body(*refs):
        kernel(*refs[:inner], *refs[inner + len(others) :])

    return pl.pallas_call(
        body,
        out_shape=out_shape,
        in_specs=[SMEM] + [HBM if first_set else VMEM] * len(operands) + [ANY] * len(others),
        out_specs=[VMEM] * len(out_shape),
        scratch_shapes=scratch,
        cost_estimate=FREE,
        compiler_params=limit(58 if first_set else 12),
        name="route",
    )(column, *operands, *others)


def hidden_tile(rows_ref, gate_ref, up_ref, hidden_ref, at, to):
    columns = pl.ds(at, TILE)
    gate = jnp.dot(rows_ref[...], gate_ref[:, columns], preferred_element_type=F32)
    upward = jnp.dot(rows_ref[...], up_ref[:, columns], preferred_element_type=F32)
    hidden_ref[:, pl.ds(to, TILE)] = (jax.nn.silu(gate) * upward).astype(BF16)


def down_chunk(hidden_ref, down_refs, chunk, width, out_refs):
    units = down_refs[0].shape[0]
    for at in range(0, width, TILE):
        columns = slice(chunk * width + at, chunk * width + at + TILE)
        total = jnp.dot(hidden_ref[:, :units], down_refs[0][:, columns], preferred_element_type=F32)
        total += jnp.dot(
            hidden_ref[:, units:], down_refs[1][:, columns], preferred_element_type=F32
        )
        for i, ref in enumerate(out_refs):
            ref[:, at : at + TILE] = total[i * CAP : (i + 1) * CAP].astype(BF16)


def expert_kernel(blocks, bring, *refs):
    rows_in, given = refs[:blocks], refs[blocks : blocks + 6]
    refs = refs[blocks + 6 :]
    outs, refs = refs[: blocks * CHUNKS], refs[blocks * CHUNKS :]
    near = given
    if bring:
        near, refs = refs[:6], refs[6:]
    rows_ref, hidden_ref = refs[:2]
    units = near[0].shape[1]
    width = outs[0].shape[1]
    copies = []

    def start(which, columns):
        if bring:
            copies.append(
                pltpu.make_async_copy(
                    given[which].at[:, columns], near[which].at[:, columns], refs[2].at[len(copies)]
                )
            )
            copies[-1].start()

    def arrived(step):
        if bring:
            copies[2 * step].wait()
            copies[2 * step + 1].wait()

    for half in range(2):
        for at in range(0, units, TILE):
            for which in (2 * half, 2 * half + 1):
                start(which, slice(at, at + TILE))
    for chunk in range(CHUNKS):
        for which in (4, 5):
            start(which, slice(chunk * width, (chunk + 1) * width))
    for i, ref in enumerate(rows_in):
        rows_ref[i * CAP : (i + 1) * CAP, :] = ref[...]
    step = 0
    for half in range(2):
        for at in range(0, units, TILE):
            arrived(step)
            hidden_tile(
                rows_ref, near[2 * half], near[2 * half + 1], hidden_ref, at, half * units + at
            )
            step += 1
    for chunk in range(CHUNKS):
        arrived(step)
        down_chunk(hidden_ref, near[4:], chunk, width, outs[chunk * blocks : (chunk + 1) * blocks])
        step += 1


def expert(rows, weights, width, bring, others=()):
    blocks, dim = len(rows), rows[0].shape[1]
    units = weights[0].shape[1]
    out_shape = [jax.ShapeDtypeStruct((CAP, width), BF16)] * (blocks * CHUNKS)
    scratch = [
        pltpu.VMEM((blocks * CAP, dim), BF16),
        pltpu.VMEM((blocks * CAP, 2 * units), BF16),
    ]
    if bring:
        out_shape += [jax.ShapeDtypeStruct(w.shape, BF16) for w in weights]
        scratch.append(pltpu.SemaphoreType.DMA((4 * (units // TILE) + 2 * CHUNKS,)))
    inner = blocks + 6

    def body(*refs):
        expert_kernel(blocks, bring, *refs[:inner], *refs[inner + len(others) :])

    outs = pl.pallas_call(
        body,
        out_shape=out_shape,
        in_specs=[VMEM] * blocks + [HBM if bring else VMEM] * 6 + [ANY] * len(others),
        out_specs=[VMEM] * len(out_shape),
        scratch_shapes=scratch,
        cost_estimate=FREE,
        compiler_params=limit(29 if bring else 12),
        name="expert",
    )(*rows, *weights, *others)
    chunks = [outs[k * blocks : (k + 1) * blocks] for k in range(CHUNKS)]
    return chunks, outs[blocks * CHUNKS :] if bring else weights


def after_kernel(*refs):
    pass


def after(values, others):
    return pl.pallas_call(
        after_kernel,
        out_shape=[jax.ShapeDtypeStruct(v.shape, v.dtype) for v in values],
        in_specs=[ANY] * (len(values) + len(others)),
        out_specs=[ANY] * len(values),
        input_output_aliases={i: i for i in range(len(values))},
        cost_estimate=FREE,
        compiler_params=limit(1),
        name="after",
    )(*values, *others)


def weighted(w_ref, kinds, refs):
    count = w_ref.shape[2] // 2
    weights = jnp.concatenate([w_ref[d] for d in kinds], axis=0)
    rows = jnp.concatenate([ref[...] for ref in refs], axis=0)
    both = lax.dot_general(weights, rows, (((0,), (0,)), ((), ())), preferred_element_type=F32)
    return both[:count] + both[count:]


def leave_kernel(swap_ref, w_own_ref, w_across_ref, *refs):
    own_refs, across_refs, out_ref = refs[:3], refs[3:6], refs[6]

    @pl.when(swap_ref[0] == 0)
    def _():
        out_ref[...] = weighted(w_across_ref, (0, 1, 3), across_refs).astype(BF16)

    @pl.when(swap_ref[0] != 0)
    def _():
        out_ref[...] = weighted(w_own_ref, (0, 1, 3), own_refs).astype(BF16)


def stay_kernel(chunk, swap_ref, w_own_ref, w_across_ref, *refs):
    own_refs, across_refs = refs[:3], refs[3:6]
    far_ref, mine_ref, tok_ref, tok_across_ref, out_ref = refs[6:]
    width = out_ref.shape[1]
    columns = slice(chunk * width, (chunk + 1) * width)

    @pl.when(swap_ref[0] == 0)
    def _():
        total = weighted(w_own_ref, (0, 1, 3, 2), (*own_refs, far_ref))
        out_ref[...] = (total + mine_ref[...].astype(F32) + tok_ref[:, columns].astype(F32)).astype(BF16)

    @pl.when(swap_ref[0] != 0)
    def _():
        total = weighted(w_across_ref, (0, 1, 3, 2), (*across_refs, far_ref))
        out_ref[...] = (
            total + mine_ref[...].astype(F32) + tok_across_ref[:, columns].astype(F32)
        ).astype(BF16)


def mix(kernel, name, swap, w_own, w_across, blocks):
    count, width = w_own.shape[2] // 2, blocks[0].shape[1]
    return pl.pallas_call(
        kernel,
        out_shape=jax.ShapeDtypeStruct((count, width), BF16),
        in_specs=[SMEM] + [VMEM] * (2 + len(blocks)),
        out_specs=VMEM,
        cost_estimate=FREE,
        compiler_params=limit(8),
        name=name,
    )(swap, w_own, w_across, *blocks)


def on_device(tokens, norm_gain, expert_ids, gate_values, gate_weight, up_weight, down_weight):
    tok = tokens[0]
    dim = tok.shape[1]
    column = lax.axis_index("expert") // 4
    swapped = lax.axis_index("section") % LAYERS == LAYERS - 1
    swap = swapped.astype(jnp.int32).reshape(1)
    column = column.astype(jnp.int32).reshape(1)
    ids = expert_ids[0].T
    gv = gate_values[0].T
    gates = (gate_weight[0], moved(gate_weight[0], 0, 0, 1))
    ups = (up_weight[0], moved(up_weight[0], 0, 0, 1))
    downs = (down_weight[0], moved(down_weight[0], 0, 0, 1))

    weights = (gates[0], ups[0], gates[1], ups[1], downs[0], downs[1])

    *own, w_own, sent = route(True, column, tok, norm_gain, (ids, gv), ())
    tok_across = moved(sent, 0, 1, 0)
    own_far = moved(own[2], 2, 0, 0)
    right_rows, left_rows = after((own[1], own[3]), (gates[1], ups[1], downs[1]))
    own_right = moved(right_rows, 1, 0, 0)
    own_left = moved(left_rows, -1, 0, 0)
    *across, w_across = route(
        False, column, tok_across, norm_gain, (), (right_rows, left_rows)
    )
    across_right = moved(across[1], 1, 0, 0)
    across_left = moved(across[2], -1, 0, 0)
    across_far = moved(own_far, 0, 1, 0)

    width = dim // CHUNKS
    first, kept = expert((own[0], own_far), weights, width, True)
    second, _ = expert((across[0], own_right, own_left, across_far), kept, width, False)
    third, _ = expert((across_right, across_left), kept, width, False, (second[-1][0],))
    outs = []
    for k in range(CHUNKS):
        own_out, far_out = first[k]
        across_out, right_out, left_out, far_late = second[k]
        right_late, left_late = third[k]
        far_in = moved(jnp.where(swapped, far_out, far_late), 0, 1, 0)
        far_kept = jnp.where(swapped, far_late, far_out)
        across_back = (across_out, moved(right_late, -1, 0, 0), moved(left_late, 1, 0, 0))
        own_back = (own_out, moved(right_out, -1, 0, 0), moved(left_out, 1, 0, 0))
        far_sum = (far_kept.astype(F32) + far_in.astype(F32)).astype(BF16)
        far_back = moved(far_sum, 2, 0, 0)
        leaving = mix(leave_kernel, "leave", swap, w_own, w_across, (*own_back, *across_back))
        mine = moved(leaving, 0, 1, 0)
        layer_out = mix(
            functools.partial(stay_kernel, k),
            "stay",
            swap,
            w_own,
            w_across,
            (*own_back, *across_back, far_back, mine, sent, tok_across),
        )
        outs.append(handed_on(layer_out))
    return jnp.concatenate(outs, axis=1)[None]


def solution(mesh):
    in_specs = (
        P("section", "expert", None),
        P("section", None),
        P("section", "expert", None),
        P("section", "expert", None),
        P("section", None, "expert"),
        P("section", None, "expert"),
        P("section", "expert", None),
    )
    out_specs = P("section", "expert", None)
    return jax.shard_map(
        on_device, mesh=mesh, in_specs=in_specs, out_specs=out_specs, check_vma=False
    )
```

```python
import functools

import jax
import jax.numpy as jnp
from jax import lax
from jax.experimental import pallas as pl
from jax.experimental.pallas import tpu as pltpu
from jax.sharding import PartitionSpec as P

EXPERTS = 4
CAP = 80
PARTS = (1792, 1792)
LAYERS = 8
TILE = 256
PACK = 128
LOAD = 46
BRING = 34
FREE = pl.CostEstimate(flops=0, bytes_accessed=0, transcendentals=0)
F32 = jnp.float32
BF16 = jnp.bfloat16
VMEM = pl.BlockSpec(memory_space=pltpu.VMEM)
SMEM = pl.BlockSpec(memory_space=pltpu.SMEM)
ANY = pl.BlockSpec(memory_space=pl.ANY)
HBM = pl.BlockSpec(memory_space=pltpu.HBM)


def limit(mebibytes):
    return pltpu.CompilerParams(vmem_limit_bytes=mebibytes << 20)


def moved(value, dx, dy, dc):
    pairs = []
    for i in range(16):
        x, y, c = i // 4, (i // 2) % 2, i % 2
        pairs.append((i, ((x + dx) % 4) * 4 + ((y + dy) % 2) * 2 + (c + dc) % 2))
    return lax.ppermute(value, "expert", pairs)


def handed_on(value):
    pairs = []
    for s in range(16):
        for e in range(16):
            to = e ^ 2 if s % LAYERS == LAYERS - 1 else e
            pairs.append((s * 16 + e, ((s + 1) % 16) * 16 + to))
    return lax.ppermute(value, ("section", "expert"), pairs)


def first_route_kernel(flags_ref, *refs):
    far, refs = refs[:4], refs[4:]
    *refs, sent_ref, gain_ref, ids_ref, gv_ref, sems = refs
    count, dim = far[0].shape
    near = (sent_ref.at[:, :dim], gain_ref, ids_ref, gv_ref)
    copies = [pltpu.make_async_copy(a, b, sems.at[i]) for i, (a, b) in enumerate(zip(far, near))]
    for copy in copies:
        copy.start()
    for copy in copies:
        copy.wait()
    ids, gv = ids_ref[...], gv_ref[...]
    high = gv.astype(BF16).astype(F32)
    middle = (gv - high).astype(BF16).astype(F32)
    low = gv - high - middle
    packed = jnp.concatenate([ids.astype(F32), high, middle, low], axis=0)
    packed = jnp.concatenate([packed, jnp.zeros((PACK - 8, count), F32)], axis=0)
    sent_ref[:, dim:] = packed.T.astype(BF16)
    route_kernel((0, 1, 2, 3), flags_ref, sent_ref, gain_ref, ids, gv, *refs)


def second_route_kernel(flags_ref, sent_ref, gain_ref, *refs):
    packed = sent_ref[:, gain_ref.shape[1] :].astype(F32).T
    ids = packed[0:2].astype(jnp.int32)
    gv = packed[2:4] + packed[4:6] + packed[6:8]
    route_kernel((0, 1, 3), flags_ref, sent_ref, gain_ref, ids, gv, *refs)


def route_kernel(kinds, flags_ref, tok_ref, gain_ref, ids, gv, *refs):
    w_ref = refs[-1]
    out_refs = dict(zip(kinds, refs[-1 - len(kinds) : -1]))
    wide = tok_ref[:, : gain_ref.shape[1]].astype(F32)
    scale = lax.rsqrt(jnp.mean(wide * wide, axis=-1, keepdims=True) + 1e-06)
    normed = (wide * scale * gain_ref[...]).astype(BF16)
    count = normed.shape[0]
    ids = jnp.bitwise_and(ids + (EXPERTS - flags_ref[0]), EXPERTS - 1)
    first, second = ids[0:1, :], ids[1:2, :]
    kind = lax.broadcasted_iota(jnp.int32, (16, count), 0)
    chosen = (kind == first) | (kind == second)
    before = (
        lax.broadcasted_iota(jnp.int32, (count, count), 0)
        < lax.broadcasted_iota(jnp.int32, (count, count), 1)
    )
    place = jnp.dot(
        chosen.astype(F32).astype(BF16), before.astype(F32).astype(BF16), preferred_element_type=F32
    )
    weight = jnp.where(kind == first, gv[0:1, :], 0.0) + jnp.where(
        kind == second, gv[1:2, :], 0.0
    )
    slot = lax.broadcasted_iota(jnp.int32, (CAP, count), 0).astype(F32)
    for d in range(EXPERTS):
        spot = jnp.where(chosen[d : d + 1, :], place[d : d + 1, :], -1.0)
        hit = slot == spot
        pick = jnp.where(hit, 1.0, 0.0).astype(BF16)
        if d in out_refs:
            out_refs[d][...] = jnp.dot(pick, normed, preferred_element_type=F32).astype(BF16)
        full = jnp.where(hit, weight[d : d + 1, :], 0.0)
        high = full.astype(BF16)
        low = (full - high.astype(F32)).astype(BF16)
        w_ref[d] = jnp.concatenate([high, low], axis=1)


def route(first_set, flags, tok, gain, choices, others):
    count, dim = tok.shape[0], gain.shape[1]
    blocks = 4 if first_set else 3
    out_shape = [jax.ShapeDtypeStruct((CAP, dim), BF16)] * blocks
    out_shape.append(jax.ShapeDtypeStruct((EXPERTS, CAP, 2 * count), BF16))
    kernel, scratch = second_route_kernel, []
    if first_set:
        kernel = first_route_kernel
        out_shape.append(jax.ShapeDtypeStruct((count, dim + PACK), BF16))
        scratch = [pltpu.VMEM(v.shape, v.dtype) for v in (gain, *choices)]
        scratch.append(pltpu.SemaphoreType.DMA((4,)))
    operands = (tok, gain, *choices)
    inner = 1 + len(operands)

    def body(*refs):
        kernel(*refs[:inner], *refs[inner + len(others) :])

    return pl.pallas_call(
        body,
        out_shape=out_shape,
        in_specs=[SMEM] + [HBM if first_set else VMEM] * len(operands) + [ANY] * len(others),
        out_specs=[VMEM] * len(out_shape),
        scratch_shapes=scratch,
        cost_estimate=FREE,
        compiler_params=limit(58 if first_set else 12),
        name="route",
    )(flags, *operands, *others)


def hidden_tile(rows_ref, gate_ref, up_ref, hidden_ref, at, to):
    columns = pl.ds(at, TILE)
    gate = jnp.dot(rows_ref[...], gate_ref[:, columns], preferred_element_type=F32)
    upward = jnp.dot(rows_ref[...], up_ref[:, columns], preferred_element_type=F32)
    hidden_ref[:, pl.ds(to, TILE)] = (jax.nn.silu(gate) * upward).astype(BF16)


def load_kernel(count, *refs):
    sems = refs[-1]
    copies = [
        pltpu.make_async_copy(refs[i], refs[i - 1 - count], sems.at[i]) for i in range(count)
    ]
    for copy in copies:
        copy.start()
    for copy in copies:
        copy.wait()


def load(weights, others, room):
    count = len(weights)
    return pl.pallas_call(
        functools.partial(load_kernel, count),
        out_shape=[jax.ShapeDtypeStruct(w.shape, BF16) for w in weights],
        in_specs=[HBM] * count + [ANY] * len(others),
        out_specs=[VMEM] * count,
        scratch_shapes=[pltpu.SemaphoreType.DMA((count,))],
        cost_estimate=FREE,
        compiler_params=limit(room),
        name="load",
    )(*weights, *others)


def expert_kernel(splits, far, flags_ref, *refs):
    blocks = len(splits)
    rows_in, weights, refs = refs[:blocks], refs[blocks : blocks + 6], refs[blocks + 6 :]
    far_refs, refs = refs[:far], refs[far:]
    *outs, rows_ref, hidden_ref = refs
    dim, units = weights[0].shape
    for i, ref in enumerate(rows_in):
        rows_ref[i * CAP : (i + 1) * CAP, :] = ref[...]
    for half in range(2):
        for at in range(0, units, TILE):
            hidden_tile(
                rows_ref, weights[3 * half], weights[3 * half + 1], hidden_ref, at, half * units + at
            )
    for at in range(0, dim, TILE):
        columns = slice(at, at + TILE)
        total = jnp.dot(
            hidden_ref[:, :units], weights[2][:, columns], preferred_element_type=F32
        ) + jnp.dot(hidden_ref[:, units:], weights[5][:, columns], preferred_element_type=F32)
        first = 0
        for i, split in enumerate(splits):
            part = total[i * CAP : (i + 1) * CAP].astype(BF16)
            chunk = sum(1 for k in range(len(split)) if at >= sum(split[: k + 1]))
            to = at - sum(split[:chunk])
            outs[first + chunk][:, to : to + TILE] = part
            first += len(split)
    if far:
        far_ref, cross_ref, kept_ref = far_refs[0], outs[0], outs[-1]

        @pl.when(flags_ref[1] == 0)
        def _():
            kept_ref[...] = far_ref[...]

        @pl.when(flags_ref[1] != 0)
        def _():
            kept_ref[...] = cross_ref[...]
            cross_ref[...] = far_ref[...]


def expert(flags, rows, weights, splits, far=(), others=()):
    blocks, dim = len(rows), rows[0].shape[1]
    units = weights[0].shape[1]
    inner = 1 + blocks + 6 + len(far)
    out_shape = [
        jax.ShapeDtypeStruct((CAP, width), BF16) for split in splits for width in split
    ] + [jax.ShapeDtypeStruct((CAP, dim), BF16)] * len(far)
    scratch = [
        pltpu.VMEM((blocks * CAP, dim), BF16),
        pltpu.VMEM((blocks * CAP, 2 * units), BF16),
    ]

    def body(*refs):
        expert_kernel(splits, len(far), *refs[:inner], *refs[inner + len(others) :])

    outs = pl.pallas_call(
        body,
        out_shape=out_shape,
        in_specs=[SMEM]
        + [VMEM] * (blocks + 6 + len(far))
        + [ANY] * len(others),
        out_specs=[VMEM] * len(out_shape),
        scratch_shapes=scratch,
        cost_estimate=FREE,
        compiler_params=limit(10),
        name="expert",
    )(flags, *rows, *weights, *far, *others)
    grouped, first = [], 0
    for split in splits:
        group = outs[first : first + len(split)]
        grouped.append(group if len(split) > 1 else group[0])
        first += len(split)
    return grouped, list(outs[first:])


def add_kernel(a_ref, b_ref, *out_refs):
    at = 0
    for ref in out_refs:
        columns = slice(at, at + ref.shape[1])
        ref[...] = (a_ref[:, columns].astype(F32) + b_ref[:, columns].astype(F32)).astype(BF16)
        at += ref.shape[1]


def added(a, b):
    return pl.pallas_call(
        add_kernel,
        out_shape=[jax.ShapeDtypeStruct((a.shape[0], width), a.dtype) for width in PARTS],
        in_specs=[VMEM] * 2,
        out_specs=[VMEM] * len(PARTS),
        cost_estimate=FREE,
        compiler_params=limit(2),
        name="add",
    )(a, b)


def after_kernel(*refs):
    pass


def after(values, others):
    return pl.pallas_call(
        after_kernel,
        out_shape=[jax.ShapeDtypeStruct(v.shape, v.dtype) for v in values],
        in_specs=[ANY] * (len(values) + len(others)),
        out_specs=[ANY] * len(values),
        input_output_aliases={i: i for i in range(len(values))},
        cost_estimate=FREE,
        compiler_params=limit(1),
        name="after",
    )(*values, *others)


def weighted(w_ref, kinds, refs, columns):
    count = w_ref.shape[2] // 2
    weights = jnp.concatenate([w_ref[d] for d in kinds], axis=0)
    width = columns.stop - columns.start
    rows = jnp.concatenate(
        [ref[...] if ref.shape[1] == width else ref[:, columns] for ref in refs], axis=0
    )
    both = lax.dot_general(weights, rows, (((0,), (0,)), ((), ())), preferred_element_type=F32)
    return both[:count] + both[count:]


def leave_kernel(columns, flags_ref, w_own_ref, w_across_ref, *refs):
    own_refs, across_refs, out_ref = refs[:3], refs[3:6], refs[6]

    @pl.when(flags_ref[1] == 0)
    def _():
        out_ref[...] = weighted(w_across_ref, (0, 1, 3), across_refs, columns).astype(BF16)

    @pl.when(flags_ref[1] != 0)
    def _():
        out_ref[...] = weighted(w_own_ref, (0, 1, 3), own_refs, columns).astype(BF16)


def stay_kernel(columns, flags_ref, w_own_ref, w_across_ref, *refs):
    own_refs, across_refs = refs[:3], refs[3:6]
    far_ref, mine_ref, tok_ref, tok_across_ref, out_ref = refs[6:]

    def finish(w_ref, near, home_ref):
        total = weighted(w_ref, (0, 1, 3, 2), (*near, far_ref), columns)
        total += mine_ref[...].astype(F32) + home_ref[:, columns].astype(F32)
        out_ref[...] = total.astype(BF16)

    @pl.when(flags_ref[1] == 0)
    def _():
        finish(w_own_ref, own_refs, tok_ref)

    @pl.when(flags_ref[1] != 0)
    def _():
        finish(w_across_ref, across_refs, tok_across_ref)


def mix(chunk, kernel, name, flags, w_own, w_across, blocks):
    count, width = w_own.shape[2] // 2, PARTS[chunk]
    begin = sum(PARTS[:chunk])
    return pl.pallas_call(
        functools.partial(kernel, slice(begin, begin + width)),
        out_shape=jax.ShapeDtypeStruct((count, width), BF16),
        in_specs=[SMEM] + [VMEM] * (2 + len(blocks)),
        out_specs=VMEM,
        cost_estimate=FREE,
        compiler_params=limit(8),
        name=name,
    )(flags, w_own, w_across, *blocks)


def on_device(tokens, norm_gain, expert_ids, gate_values, gate_weight, up_weight, down_weight):
    tok = tokens[0]
    dim = tok.shape[1]
    column = lax.axis_index("expert") // 4
    swapped = lax.axis_index("section") % LAYERS == LAYERS - 1
    flags = jnp.stack([column.astype(jnp.int32), swapped.astype(jnp.int32)])
    ids = expert_ids[0].T
    gv = gate_values[0].T
    gates = (gate_weight[0], moved(gate_weight[0], 0, 0, 1))
    ups = (up_weight[0], moved(up_weight[0], 0, 0, 1))
    downs = (down_weight[0], moved(down_weight[0], 0, 0, 1))

    *own, w_own, sent = route(True, flags, tok, norm_gain, (ids, gv), ())
    tok_across = moved(sent, 0, 1, 0)
    own_far = moved(own[2], 2, 0, 0)
    held = load((gates[0], ups[0], downs[0]), (sent,), LOAD)
    right_rows, left_rows = after((own[1], own[3]), (gates[1], ups[1], downs[1], held[0]))
    own_right = moved(right_rows, 1, 0, 0)
    own_left = moved(left_rows, -1, 0, 0)
    held_more = load((gates[1], ups[1], downs[1]), (own_far,), BRING)
    (own_far,) = after((own_far,), (right_rows, left_rows, tok_across))
    across_far = moved(own_far, 0, 1, 0)
    kept = (*held, *held_more)
    whole, split = (dim,), PARTS
    *across, w_across = route(False, flags, tok_across, norm_gain, (), (kept[3],))
    (own_out, far_out, right_out, left_out), _ = expert(
        flags, (own[0], own_far, own_right, own_left), kept, (whole,) * 4
    )
    across_right = moved(across[1], 1, 0, 0)
    across_left = moved(across[2], -1, 0, 0)
    (far_cross, across_out), (far_kept,) = expert(
        flags, (across_far, across[0]), kept, (whole,) * 2, (far_out,)
    )
    (right_late, left_late), _ = expert(
        flags, (across_right, across_left), kept, (split,) * 2, others=(far_cross,)
    )
    my_right = moved(right_out, -1, 0, 0)
    my_left = moved(left_out, 1, 0, 0)
    far_in = moved(far_cross, 0, 1, 0)
    sums = added(far_kept, far_in)
    outs = []
    for k in range(len(PARTS)):
        right_rows, left_rows = right_late[k], left_late[k]
        if k > 0:
            right_rows, left_rows = after((right_rows, left_rows), (my_right, my_left))
        own_back = (own_out, my_right, my_left)
        across_back = (across_out, moved(right_rows, -1, 0, 0), moved(left_rows, 1, 0, 0))
        far_back = moved(sums[k], 2, 0, 0)
        leaving = mix(k, leave_kernel, "leave", flags, w_own, w_across, (*own_back, *across_back))
        if k > 0:
            (leaving,) = after((leaving,), (arrived,))
        mine, arrived = moved(leaving, 0, 1, 0), far_back
        layer_out = mix(
            k,
            stay_kernel,
            "stay",
            flags,
            w_own,
            w_across,
            (*own_back, *across_back, far_back, mine, sent, tok_across),
        )
        outs.append(handed_on(layer_out))
    return jnp.concatenate(outs, axis=1)[None]


def solution(mesh):
    in_specs = (
        P("section", "expert", None),
        P("section", None),
        P("section", "expert", None),
        P("section", "expert", None),
        P("section", None, "expert"),
        P("section", None, "expert"),
        P("section", "expert", None),
    )
    out_specs = P("section", "expert", None)
    return jax.shard_map(
        on_device, mesh=mesh, in_specs=in_specs, out_specs=out_specs, check_vma=False
    )
```

```python
import functools

import jax
import jax.numpy as jnp
from jax import lax
from jax.experimental import pallas as pl
from jax.experimental.pallas import tpu as pltpu
from jax.sharding import PartitionSpec as P

EXPERTS = 4
CAP = 80
PARTS = (1792, 1792)
LAYERS = 8
TILE = 256
PACK = 128
LOAD = 46
BRING = 34
FREE = pl.CostEstimate(flops=0, bytes_accessed=0, transcendentals=0)
F32 = jnp.float32
BF16 = jnp.bfloat16
VMEM = pl.BlockSpec(memory_space=pltpu.VMEM)
ANY = pl.BlockSpec(memory_space=pl.ANY)
HBM = pl.BlockSpec(memory_space=pltpu.HBM)


def limit(mebibytes):
    return pltpu.CompilerParams(vmem_limit_bytes=mebibytes << 20)


def column():
    return lax.axis_index("expert") // 4


def swapped():
    return lax.axis_index("section") % LAYERS == LAYERS - 1


def moved(value, dx, dy, dc):
    pairs = []
    for i in range(16):
        x, y, c = i // 4, (i // 2) % 2, i % 2
        pairs.append((i, ((x + dx) % 4) * 4 + ((y + dy) % 2) * 2 + (c + dc) % 2))
    return lax.ppermute(value, "expert", pairs)


def handed_on(value):
    pairs = []
    for s in range(16):
        for e in range(16):
            to = e ^ 2 if s % LAYERS == LAYERS - 1 else e
            pairs.append((s * 16 + e, ((s + 1) % 16) * 16 + to))
    return lax.ppermute(value, ("section", "expert"), pairs)


def first_route_kernel(*refs):
    far, refs = refs[:4], refs[4:]
    *refs, sent_ref, gain_ref, ids_ref, gv_ref, sems = refs
    count, dim = far[0].shape
    near = (sent_ref.at[:, :dim], gain_ref, ids_ref, gv_ref)
    copies = [pltpu.make_async_copy(a, b, sems.at[i]) for i, (a, b) in enumerate(zip(far, near))]
    for copy in copies:
        copy.start()
    for copy in copies:
        copy.wait()
    ids, gv = ids_ref[...], gv_ref[...]
    high = gv.astype(BF16).astype(F32)
    middle = (gv - high).astype(BF16).astype(F32)
    low = gv - high - middle
    packed = jnp.concatenate([ids.astype(F32), high, middle, low], axis=0)
    packed = jnp.concatenate([packed, jnp.zeros((PACK - 8, count), F32)], axis=0)
    sent_ref[:, dim:] = packed.T.astype(BF16)
    route_kernel((0, 1, 2, 3), sent_ref, gain_ref, ids, gv, *refs)


def second_route_kernel(sent_ref, gain_ref, *refs):
    packed = sent_ref[:, gain_ref.shape[1] :].astype(F32).T
    ids = packed[0:2].astype(jnp.int32)
    gv = packed[2:4] + packed[4:6] + packed[6:8]
    route_kernel((0, 1, 3), sent_ref, gain_ref, ids, gv, *refs)


def route_kernel(kinds, tok_ref, gain_ref, ids, gv, *refs):
    w_ref = refs[-1]
    out_refs = dict(zip(kinds, refs[-1 - len(kinds) : -1]))
    wide = tok_ref[:, : gain_ref.shape[1]].astype(F32)
    scale = lax.rsqrt(jnp.mean(wide * wide, axis=-1, keepdims=True) + 1e-06)
    normed = (wide * scale * gain_ref[...]).astype(BF16)
    count = normed.shape[0]
    ids = jnp.bitwise_and(ids + (EXPERTS - column()), EXPERTS - 1)
    first, second = ids[0:1, :], ids[1:2, :]
    kind = lax.broadcasted_iota(jnp.int32, (16, count), 0)
    chosen = (kind == first) | (kind == second)
    before = (
        lax.broadcasted_iota(jnp.int32, (count, count), 0)
        < lax.broadcasted_iota(jnp.int32, (count, count), 1)
    )
    place = jnp.dot(
        chosen.astype(F32).astype(BF16), before.astype(F32).astype(BF16), preferred_element_type=F32
    )
    weight = jnp.where(kind == first, gv[0:1, :], 0.0) + jnp.where(
        kind == second, gv[1:2, :], 0.0
    )
    slot = lax.broadcasted_iota(jnp.int32, (CAP, count), 0).astype(F32)
    for d in range(EXPERTS):
        spot = jnp.where(chosen[d : d + 1, :], place[d : d + 1, :], -1.0)
        hit = slot == spot
        pick = jnp.where(hit, 1.0, 0.0).astype(BF16)
        if d in out_refs:
            out_refs[d][...] = jnp.dot(pick, normed, preferred_element_type=F32).astype(BF16)
        full = jnp.where(hit, weight[d : d + 1, :], 0.0)
        high = full.astype(BF16)
        low = (full - high.astype(F32)).astype(BF16)
        w_ref[d] = jnp.concatenate([high, low], axis=1)


def route(first_set, tok, gain, choices, others):
    count, dim = tok.shape[0], gain.shape[1]
    blocks = 4 if first_set else 3
    out_shape = [jax.ShapeDtypeStruct((CAP, dim), BF16)] * blocks
    out_shape.append(jax.ShapeDtypeStruct((EXPERTS, CAP, 2 * count), BF16))
    kernel, scratch = second_route_kernel, []
    if first_set:
        kernel = first_route_kernel
        out_shape.append(jax.ShapeDtypeStruct((count, dim + PACK), BF16))
        scratch = [pltpu.VMEM(v.shape, v.dtype) for v in (gain, *choices)]
        scratch.append(pltpu.SemaphoreType.DMA((4,)))
    operands = (tok, gain, *choices)
    inner = len(operands)

    def body(*refs):
        kernel(*refs[:inner], *refs[inner + len(others) :])

    return pl.pallas_call(
        body,
        out_shape=out_shape,
        in_specs=[HBM if first_set else VMEM] * len(operands) + [ANY] * len(others),
        out_specs=[VMEM] * len(out_shape),
        scratch_shapes=scratch,
        cost_estimate=FREE,
        compiler_params=limit(58 if first_set else 12),
        name="route",
    )(*operands, *others)


def hidden_tile(rows_ref, gate_ref, up_ref, hidden_ref, at, to):
    columns = pl.ds(at, TILE)
    gate = jnp.dot(rows_ref[...], gate_ref[:, columns], preferred_element_type=F32)
    upward = jnp.dot(rows_ref[...], up_ref[:, columns], preferred_element_type=F32)
    hidden_ref[:, pl.ds(to, TILE)] = (jax.nn.silu(gate) * upward).astype(BF16)


def load_kernel(count, *refs):
    sems = refs[-1]
    copies = [
        pltpu.make_async_copy(refs[i], refs[i - 1 - count], sems.at[i]) for i in range(count)
    ]
    for copy in copies:
        copy.start()
    for copy in copies:
        copy.wait()


def load(weights, others, room):
    count = len(weights)
    return pl.pallas_call(
        functools.partial(load_kernel, count),
        out_shape=[jax.ShapeDtypeStruct(w.shape, BF16) for w in weights],
        in_specs=[HBM] * count + [ANY] * len(others),
        out_specs=[VMEM] * count,
        scratch_shapes=[pltpu.SemaphoreType.DMA((count,))],
        cost_estimate=FREE,
        compiler_params=limit(room),
        name="load",
    )(*weights, *others)


def expert_kernel(splits, far, *refs):
    blocks = len(splits)
    rows_in, weights, refs = refs[:blocks], refs[blocks : blocks + 6], refs[blocks + 6 :]
    far_refs, refs = refs[:far], refs[far:]
    *outs, rows_ref, hidden_ref = refs
    dim, units = weights[0].shape
    for i, ref in enumerate(rows_in):
        rows_ref[i * CAP : (i + 1) * CAP, :] = ref[...]
    for half in range(2):
        for at in range(0, units, TILE):
            hidden_tile(
                rows_ref, weights[3 * half], weights[3 * half + 1], hidden_ref, at, half * units + at
            )
    for at in range(0, dim, TILE):
        columns = slice(at, at + TILE)
        total = jnp.dot(
            hidden_ref[:, :units], weights[2][:, columns], preferred_element_type=F32
        ) + jnp.dot(hidden_ref[:, units:], weights[5][:, columns], preferred_element_type=F32)
        first = 0
        for i, split in enumerate(splits):
            part = total[i * CAP : (i + 1) * CAP].astype(BF16)
            chunk = sum(1 for k in range(len(split)) if at >= sum(split[: k + 1]))
            to = at - sum(split[:chunk])
            outs[first + chunk][:, to : to + TILE] = part
            first += len(split)
    if far:
        far_ref, cross_ref, kept_ref = far_refs[0], outs[0], outs[-1]

        @pl.when(jnp.logical_not(swapped()))
        def _():
            kept_ref[...] = far_ref[...]

        @pl.when(swapped())
        def _():
            kept_ref[...] = cross_ref[...]
            cross_ref[...] = far_ref[...]


def expert(rows, weights, splits, far=(), others=()):
    blocks, dim = len(rows), rows[0].shape[1]
    units = weights[0].shape[1]
    inner = blocks + 6 + len(far)
    out_shape = [
        jax.ShapeDtypeStruct((CAP, width), BF16) for split in splits for width in split
    ] + [jax.ShapeDtypeStruct((CAP, dim), BF16)] * len(far)
    scratch = [
        pltpu.VMEM((blocks * CAP, dim), BF16),
        pltpu.VMEM((blocks * CAP, 2 * units), BF16),
    ]

    def body(*refs):
        expert_kernel(splits, len(far), *refs[:inner], *refs[inner + len(others) :])

    outs = pl.pallas_call(
        body,
        out_shape=out_shape,
        in_specs=[VMEM] * inner
        + [ANY] * len(others),
        out_specs=[VMEM] * len(out_shape),
        scratch_shapes=scratch,
        cost_estimate=FREE,
        compiler_params=limit(10),
        name="expert",
    )(*rows, *weights, *far, *others)
    grouped, first = [], 0
    for split in splits:
        group = outs[first : first + len(split)]
        grouped.append(group if len(split) > 1 else group[0])
        first += len(split)
    return grouped, list(outs[first:])


def add_kernel(a_ref, b_ref, *out_refs):
    at = 0
    for ref in out_refs:
        columns = slice(at, at + ref.shape[1])
        ref[...] = (a_ref[:, columns].astype(F32) + b_ref[:, columns].astype(F32)).astype(BF16)
        at += ref.shape[1]


def added(a, b):
    return pl.pallas_call(
        add_kernel,
        out_shape=[jax.ShapeDtypeStruct((a.shape[0], width), a.dtype) for width in PARTS],
        in_specs=[VMEM] * 2,
        out_specs=[VMEM] * len(PARTS),
        cost_estimate=FREE,
        compiler_params=limit(2),
        name="add",
    )(a, b)


def after_kernel(*refs):
    pass


def after(values, others):
    return pl.pallas_call(
        after_kernel,
        out_shape=[jax.ShapeDtypeStruct(v.shape, v.dtype) for v in values],
        in_specs=[ANY] * (len(values) + len(others)),
        out_specs=[ANY] * len(values),
        input_output_aliases={i: i for i in range(len(values))},
        cost_estimate=FREE,
        compiler_params=limit(1),
        name="after",
    )(*values, *others)


def weighted(w_ref, kinds, refs, columns):
    count = w_ref.shape[2] // 2
    weights = jnp.concatenate([w_ref[d] for d in kinds], axis=0)
    width = columns.stop - columns.start
    rows = jnp.concatenate(
        [ref[...] if ref.shape[1] == width else ref[:, columns] for ref in refs], axis=0
    )
    both = lax.dot_general(weights, rows, (((0,), (0,)), ((), ())), preferred_element_type=F32)
    return both[:count] + both[count:]


def leave_kernel(columns, w_own_ref, w_across_ref, *refs):
    own_refs, across_refs, out_ref = refs[:3], refs[3:6], refs[6]

    @pl.when(jnp.logical_not(swapped()))
    def _():
        out_ref[...] = weighted(w_across_ref, (0, 1, 3), across_refs, columns).astype(BF16)

    @pl.when(swapped())
    def _():
        out_ref[...] = weighted(w_own_ref, (0, 1, 3), own_refs, columns).astype(BF16)


def stay_kernel(columns, w_own_ref, w_across_ref, *refs):
    own_refs, across_refs = refs[:3], refs[3:6]
    far_ref, mine_ref, tok_ref, tok_across_ref, out_ref = refs[6:]

    def finish(w_ref, near, home_ref):
        total = weighted(w_ref, (0, 1, 3, 2), (*near, far_ref), columns)
        total += mine_ref[...].astype(F32) + home_ref[:, columns].astype(F32)
        out_ref[...] = total.astype(BF16)

    @pl.when(jnp.logical_not(swapped()))
    def _():
        finish(w_own_ref, own_refs, tok_ref)

    @pl.when(swapped())
    def _():
        finish(w_across_ref, across_refs, tok_across_ref)


def mix(chunk, kernel, name, w_own, w_across, blocks):
    count, width = w_own.shape[2] // 2, PARTS[chunk]
    begin = sum(PARTS[:chunk])
    return pl.pallas_call(
        functools.partial(kernel, slice(begin, begin + width)),
        out_shape=jax.ShapeDtypeStruct((count, width), BF16),
        in_specs=[VMEM] * (2 + len(blocks)),
        out_specs=VMEM,
        cost_estimate=FREE,
        compiler_params=limit(8),
        name=name,
    )(w_own, w_across, *blocks)


def on_device(tokens, norm_gain, expert_ids, gate_values, gate_weight, up_weight, down_weight):
    tok = tokens[0]
    dim = tok.shape[1]
    ids = expert_ids[0].T
    gv = gate_values[0].T
    gates = (gate_weight[0], moved(gate_weight[0], 0, 0, 1))
    ups = (up_weight[0], moved(up_weight[0], 0, 0, 1))
    downs = (down_weight[0], moved(down_weight[0], 0, 0, 1))

    *own, w_own, sent = route(True, tok, norm_gain, (ids, gv), ())
    tok_across = moved(sent, 0, 1, 0)
    own_far = moved(own[2], 2, 0, 0)
    held = load((gates[0], ups[0], downs[0]), (sent,), LOAD)
    right_rows, left_rows = after((own[1], own[3]), (gates[1], ups[1], downs[1], held[0]))
    own_right = moved(right_rows, 1, 0, 0)
    own_left = moved(left_rows, -1, 0, 0)
    held_more = load((gates[1], ups[1], downs[1]), (own_far,), BRING)
    (own_far,) = after((own_far,), (right_rows, left_rows, tok_across))
    across_far = moved(own_far, 0, 1, 0)
    kept = (*held, *held_more)
    whole, split = (dim,), PARTS
    *across, w_across = route(False, tok_across, norm_gain, (), (kept[3],))
    (own_out, far_out, right_out, left_out), _ = expert(
        (own[0], own_far, own_right, own_left), kept, (whole,) * 4
    )
    across_right = moved(across[1], 1, 0, 0)
    across_left = moved(across[2], -1, 0, 0)
    (far_cross, across_out), (far_kept,) = expert(
        (across_far, across[0]), kept, (whole,) * 2, (far_out,)
    )
    (right_late, left_late), _ = expert(
        (across_right, across_left), kept, (split,) * 2, others=(far_cross,)
    )
    my_right = moved(right_out, -1, 0, 0)
    my_left = moved(left_out, 1, 0, 0)
    far_in = moved(far_cross, 0, 1, 0)
    sums = added(far_kept, far_in)
    outs = []
    for k in range(len(PARTS)):
        right_rows, left_rows = right_late[k], left_late[k]
        if k > 0:
            right_rows, left_rows = after((right_rows, left_rows), (my_right, my_left))
        own_back = (own_out, my_right, my_left)
        across_back = (across_out, moved(right_rows, -1, 0, 0), moved(left_rows, 1, 0, 0))
        far_back = moved(sums[k], 2, 0, 0)
        leaving = mix(k, leave_kernel, "leave", w_own, w_across, (*own_back, *across_back))
        if k > 0:
            (leaving,) = after((leaving,), (arrived,))
        mine, arrived = moved(leaving, 0, 1, 0), far_back
        layer_out = mix(
            k,
            stay_kernel,
            "stay",
            w_own,
            w_across,
            (*own_back, *across_back, far_back, mine, sent, tok_across),
        )
        outs.append(handed_on(layer_out))
    return jnp.concatenate(outs, axis=1)[None]


def solution(mesh):
    in_specs = (
        P("section", "expert", None),
        P("section", None),
        P("section", "expert", None),
        P("section", "expert", None),
        P("section", None, "expert"),
        P("section", None, "expert"),
        P("section", "expert", None),
    )
    out_specs = P("section", "expert", None)
    return jax.shard_map(
        on_device, mesh=mesh, in_specs=in_specs, out_specs=out_specs, check_vma=False
    )
```

```python
import functools

import jax
import jax.numpy as jnp
from jax import lax
from jax.experimental import pallas as pl
from jax.experimental.pallas import tpu as pltpu
from jax.sharding import PartitionSpec as P

EXPERTS = 4
CAP = 80
PARTS = (1792, 1792)
LAYERS = 8
TILE = 256
PACK = 128
LOAD = 46
BRING = 34
FREE = pl.CostEstimate(flops=0, bytes_accessed=0, transcendentals=0)
F32 = jnp.float32
BF16 = jnp.bfloat16
VMEM = pl.BlockSpec(memory_space=pltpu.VMEM)
ANY = pl.BlockSpec(memory_space=pl.ANY)
HBM = pl.BlockSpec(memory_space=pltpu.HBM)


def limit(mebibytes):
    return pltpu.CompilerParams(vmem_limit_bytes=mebibytes << 20)


def column():
    return lax.axis_index("expert") // 4


def swapped():
    return lax.axis_index("section") % LAYERS == LAYERS - 1


def moved(value, dx, dy, dc):
    pairs = []
    for i in range(16):
        x, y, c = i // 4, (i // 2) % 2, i % 2
        pairs.append((i, ((x + dx) % 4) * 4 + ((y + dy) % 2) * 2 + (c + dc) % 2))
    return lax.ppermute(value, "expert", pairs)


def handed_on(value):
    pairs = []
    for s in range(16):
        for e in range(16):
            to = e ^ 2 if s % LAYERS == LAYERS - 1 else e
            pairs.append((s * 16 + e, ((s + 1) % 16) * 16 + to))
    return lax.ppermute(value, ("section", "expert"), pairs)


def first_route_kernel(*refs):
    far, refs = refs[:4], refs[4:]
    *refs, sent_ref, gain_ref, ids_ref, gv_ref, sems = refs
    count, dim = far[0].shape
    near = (sent_ref.at[:, :dim], gain_ref, ids_ref, gv_ref)
    copies = [pltpu.make_async_copy(a, b, sems.at[i]) for i, (a, b) in enumerate(zip(far, near))]
    for copy in copies:
        copy.start()
    for copy in copies:
        copy.wait()
    ids, gv = ids_ref[...], gv_ref[...]
    high = gv.astype(BF16).astype(F32)
    middle = (gv - high).astype(BF16).astype(F32)
    low = gv - high - middle
    packed = jnp.concatenate([ids.astype(F32), high, middle, low], axis=0)
    packed = jnp.concatenate([packed, jnp.zeros((PACK - 8, count), F32)], axis=0)
    sent_ref[:, dim:] = packed.T.astype(BF16)
    route_kernel((0, 1, 2, 3), sent_ref, gain_ref, ids, gv, *refs)


def second_route_kernel(sent_ref, gain_ref, *refs):
    packed = sent_ref[:, gain_ref.shape[1] :].astype(F32).T
    ids = packed[0:2].astype(jnp.int32)
    gv = packed[2:4] + packed[4:6] + packed[6:8]
    route_kernel((0, 1, 3), sent_ref, gain_ref, ids, gv, *refs)


def route_kernel(kinds, tok_ref, gain_ref, ids, gv, *refs):
    w_ref = refs[-1]
    out_refs = dict(zip(kinds, refs[-1 - len(kinds) : -1]))
    wide = tok_ref[:, : gain_ref.shape[1]].astype(F32)
    scale = lax.rsqrt(jnp.mean(wide * wide, axis=-1, keepdims=True) + 1e-06)
    normed = (wide * scale * gain_ref[...]).astype(BF16)
    count = normed.shape[0]
    ids = jnp.bitwise_and(ids + (EXPERTS - column()), EXPERTS - 1)
    first, second = ids[0:1, :], ids[1:2, :]
    kind = lax.broadcasted_iota(jnp.int32, (16, count), 0)
    chosen = (kind == first) | (kind == second)
    before = (
        lax.broadcasted_iota(jnp.int32, (count, count), 0)
        < lax.broadcasted_iota(jnp.int32, (count, count), 1)
    )
    place = jnp.dot(
        chosen.astype(F32).astype(BF16), before.astype(F32).astype(BF16), preferred_element_type=F32
    )
    weight = jnp.where(kind == first, gv[0:1, :], 0.0) + jnp.where(
        kind == second, gv[1:2, :], 0.0
    )
    slot = lax.broadcasted_iota(jnp.int32, (CAP, count), 0).astype(F32)
    for d in range(EXPERTS):
        spot = jnp.where(chosen[d : d + 1, :], place[d : d + 1, :], -1.0)
        hit = slot == spot
        pick = jnp.where(hit, 1.0, 0.0).astype(BF16)
        if d in out_refs:
            out_refs[d][...] = jnp.dot(pick, normed, preferred_element_type=F32).astype(BF16)
        full = jnp.where(hit, weight[d : d + 1, :], 0.0)
        high = full.astype(BF16)
        low = (full - high.astype(F32)).astype(BF16)
        w_ref[d] = jnp.concatenate([high, low], axis=1)


def route(first_set, tok, gain, choices, others):
    count, dim = tok.shape[0], gain.shape[1]
    blocks = 4 if first_set else 3
    out_shape = [jax.ShapeDtypeStruct((CAP, dim), BF16)] * blocks
    out_shape.append(jax.ShapeDtypeStruct((EXPERTS, CAP, 2 * count), BF16))
    kernel, scratch = second_route_kernel, []
    if first_set:
        kernel = first_route_kernel
        out_shape.append(jax.ShapeDtypeStruct((count, dim + PACK), BF16))
        scratch = [pltpu.VMEM(v.shape, v.dtype) for v in (gain, *choices)]
        scratch.append(pltpu.SemaphoreType.DMA((4,)))
    operands = (tok, gain, *choices)
    inner = len(operands)

    def body(*refs):
        kernel(*refs[:inner], *refs[inner + len(others) :])

    return pl.pallas_call(
        body,
        out_shape=out_shape,
        in_specs=[HBM if first_set else VMEM] * len(operands) + [ANY] * len(others),
        out_specs=[VMEM] * len(out_shape),
        scratch_shapes=scratch,
        cost_estimate=FREE,
        compiler_params=limit(58 if first_set else 12),
        name="route",
    )(*operands, *others)


def hidden_tile(rows_ref, gate_ref, up_ref, hidden_ref, at, to):
    columns = pl.ds(at, TILE)
    gate = jnp.dot(rows_ref[...], gate_ref[:, columns], preferred_element_type=F32)
    upward = jnp.dot(rows_ref[...], up_ref[:, columns], preferred_element_type=F32)
    hidden_ref[:, pl.ds(to, TILE)] = (jax.nn.silu(gate) * upward).astype(BF16)


def load_kernel(count, *refs):
    sems = refs[-1]
    copies = [
        pltpu.make_async_copy(refs[i], refs[i - 1 - count], sems.at[i]) for i in range(count)
    ]
    for copy in copies:
        copy.start()
    for copy in copies:
        copy.wait()


def load(weights, others, room):
    count = len(weights)
    return pl.pallas_call(
        functools.partial(load_kernel, count),
        out_shape=[jax.ShapeDtypeStruct(w.shape, BF16) for w in weights],
        in_specs=[HBM] * count + [ANY] * len(others),
        out_specs=[VMEM] * count,
        scratch_shapes=[pltpu.SemaphoreType.DMA((count,))],
        cost_estimate=FREE,
        compiler_params=limit(room),
        name="load",
    )(*weights, *others)


def expert_kernel(splits, far, *refs):
    blocks = len(splits)
    rows_in, weights, refs = refs[:blocks], refs[blocks : blocks + 6], refs[blocks + 6 :]
    far_refs, refs = refs[:far], refs[far:]
    *outs, rows_ref, hidden_ref = refs
    dim, units = weights[0].shape
    for i, ref in enumerate(rows_in):
        rows_ref[i * CAP : (i + 1) * CAP, :] = ref[...]
    for half in range(2):
        for at in range(0, units, TILE):
            hidden_tile(
                rows_ref, weights[3 * half], weights[3 * half + 1], hidden_ref, at, half * units + at
            )
    for at in range(0, dim, TILE):
        columns = slice(at, at + TILE)
        total = jnp.dot(
            hidden_ref[:, :units], weights[2][:, columns], preferred_element_type=F32
        ) + jnp.dot(hidden_ref[:, units:], weights[5][:, columns], preferred_element_type=F32)
        first = 0
        for i, split in enumerate(splits):
            part = total[i * CAP : (i + 1) * CAP].astype(BF16)
            chunk = sum(1 for k in range(len(split)) if at >= sum(split[: k + 1]))
            to = at - sum(split[:chunk])
            outs[first + chunk][:, to : to + TILE] = part
            first += len(split)
    if far:
        far_ref, cross_ref, kept_ref = far_refs[0], outs[0], outs[-1]

        @pl.when(jnp.logical_not(swapped()))
        def _():
            kept_ref[...] = far_ref[...]

        @pl.when(swapped())
        def _():
            kept_ref[...] = cross_ref[...]
            cross_ref[...] = far_ref[...]


def expert(rows, weights, splits, far=(), others=()):
    blocks, dim = len(rows), rows[0].shape[1]
    units = weights[0].shape[1]
    inner = blocks + 6 + len(far)
    out_shape = [
        jax.ShapeDtypeStruct((CAP, width), BF16) for split in splits for width in split
    ] + [jax.ShapeDtypeStruct((CAP, dim), BF16)] * len(far)
    scratch = [
        pltpu.VMEM((blocks * CAP, dim), BF16),
        pltpu.VMEM((blocks * CAP, 2 * units), BF16),
    ]

    def body(*refs):
        expert_kernel(splits, len(far), *refs[:inner], *refs[inner + len(others) :])

    outs = pl.pallas_call(
        body,
        out_shape=out_shape,
        in_specs=[VMEM] * inner
        + [ANY] * len(others),
        out_specs=[VMEM] * len(out_shape),
        scratch_shapes=scratch,
        cost_estimate=FREE,
        compiler_params=limit(10),
        name="expert",
    )(*rows, *weights, *far, *others)
    grouped, first = [], 0
    for split in splits:
        group = outs[first : first + len(split)]
        grouped.append(group if len(split) > 1 else group[0])
        first += len(split)
    return grouped, list(outs[first:])


def add_kernel(a_ref, b_ref, *out_refs):
    at = 0
    for ref in out_refs:
        columns = slice(at, at + ref.shape[1])
        ref[...] = (a_ref[:, columns].astype(F32) + b_ref[:, columns].astype(F32)).astype(BF16)
        at += ref.shape[1]


def added(a, b):
    return pl.pallas_call(
        add_kernel,
        out_shape=[jax.ShapeDtypeStruct((a.shape[0], width), a.dtype) for width in PARTS],
        in_specs=[VMEM] * 2,
        out_specs=[VMEM] * len(PARTS),
        cost_estimate=FREE,
        compiler_params=limit(2),
        name="add",
    )(a, b)


def after_kernel(*refs):
    pass


def after(values, others):
    return pl.pallas_call(
        after_kernel,
        out_shape=[jax.ShapeDtypeStruct(v.shape, v.dtype) for v in values],
        in_specs=[ANY] * (len(values) + len(others)),
        out_specs=[ANY] * len(values),
        input_output_aliases={i: i for i in range(len(values))},
        cost_estimate=FREE,
        compiler_params=limit(1),
        name="after",
    )(*values, *others)


def weighted(w_ref, kinds, refs, columns):
    count = w_ref.shape[2] // 2
    weights = jnp.concatenate([w_ref[d] for d in kinds], axis=0)
    width = columns.stop - columns.start
    rows = jnp.concatenate(
        [ref[...] if ref.shape[1] == width else ref[:, columns] for ref in refs], axis=0
    )
    both = lax.dot_general(weights, rows, (((0,), (0,)), ((), ())), preferred_element_type=F32)
    return both[:count] + both[count:]


def leave_kernel(columns, w_own_ref, w_across_ref, *refs):
    own_refs, across_refs, out_ref = refs[:3], refs[3:6], refs[6]

    @pl.when(jnp.logical_not(swapped()))
    def _():
        out_ref[...] = weighted(w_across_ref, (0, 1, 3), across_refs, columns).astype(BF16)

    @pl.when(swapped())
    def _():
        out_ref[...] = weighted(w_own_ref, (0, 1, 3), own_refs, columns).astype(BF16)


def stay_kernel(columns, w_own_ref, w_across_ref, *refs):
    own_refs, across_refs = refs[:3], refs[3:6]
    far_ref, mine_ref, tok_ref, tok_across_ref, out_ref = refs[6:]

    def finish(w_ref, near, home_ref):
        total = weighted(w_ref, (0, 1, 3, 2), (*near, far_ref), columns)
        total += mine_ref[...].astype(F32) + home_ref[:, columns].astype(F32)
        out_ref[...] = total.astype(BF16)

    @pl.when(jnp.logical_not(swapped()))
    def _():
        finish(w_own_ref, own_refs, tok_ref)

    @pl.when(swapped())
    def _():
        finish(w_across_ref, across_refs, tok_across_ref)


def mix(chunk, kernel, name, w_own, w_across, blocks):
    count, width = w_own.shape[2] // 2, PARTS[chunk]
    begin = sum(PARTS[:chunk])
    return pl.pallas_call(
        functools.partial(kernel, slice(begin, begin + width)),
        out_shape=jax.ShapeDtypeStruct((count, width), BF16),
        in_specs=[VMEM] * (2 + len(blocks)),
        out_specs=VMEM,
        cost_estimate=FREE,
        compiler_params=limit(8),
        name=name,
    )(w_own, w_across, *blocks)


def on_device(tokens, norm_gain, expert_ids, gate_values, gate_weight, up_weight, down_weight):
    tok = tokens[0]
    dim = tok.shape[1]
    ids = expert_ids[0].T
    gv = gate_values[0].T
    gates = (gate_weight[0], moved(gate_weight[0], 0, 0, 1))
    ups = (up_weight[0], moved(up_weight[0], 0, 0, 1))
    downs = (down_weight[0], moved(down_weight[0], 0, 0, 1))

    *own, w_own, sent = route(True, tok, norm_gain, (ids, gv), ())
    tok_across = moved(sent, 0, 1, 0)
    own_far = moved(own[2], 2, 0, 0)
    held = load((gates[0], ups[0], downs[0]), (sent,), LOAD)
    right_rows, left_rows = after((own[1], own[3]), (gates[1], ups[1], downs[1], held[0]))
    own_right = moved(right_rows, 1, 0, 0)
    own_left = moved(left_rows, -1, 0, 0)
    held_more = load((gates[1], ups[1], downs[1]), (own_far,), BRING)
    (own_far,) = after((own_far,), (right_rows, left_rows, tok_across))
    across_far = moved(own_far, 0, 1, 0)
    kept = (*held, *held_more)
    whole, split = (dim,), PARTS
    *across, w_across = route(False, tok_across, norm_gain, (), (kept[3],))
    (own_out, far_out, right_out, left_out), _ = expert(
        (own[0], own_far, own_right, own_left), kept, (whole,) * 4
    )
    across_right = moved(across[1], 1, 0, 0)
    across_left = moved(across[2], -1, 0, 0)
    (far_cross, across_out), (far_kept,) = expert(
        (across_far, across[0]), kept, (whole,) * 2, (far_out,)
    )
    (right_late, left_late), _ = expert(
        (across_right, across_left), kept, (split,) * 2, others=(far_cross,)
    )
    my_right = moved(right_out, -1, 0, 0)
    my_left = moved(left_out, 1, 0, 0)
    far_in = moved(far_cross, 0, 1, 0)
    sums = added(far_kept, far_in)
    outs = []
    for k in range(len(PARTS)):
        right_rows, left_rows = right_late[k], left_late[k]
        if k > 0:
            right_rows, left_rows = after((right_rows, left_rows), (my_right, my_left))
        own_back = (own_out, my_right, my_left)
        across_back = (across_out, moved(right_rows, -1, 0, 0), moved(left_rows, 1, 0, 0))
        far_rows = sums[k]
        if k > 0:
            (far_rows,) = after((far_rows,), (arrived,))
        far_back = moved(far_rows, 2, 0, 0)
        leaving = mix(k, leave_kernel, "leave", w_own, w_across, (*own_back, *across_back))
        mine, arrived = moved(leaving, 0, 1, 0), far_back
        layer_out = mix(
            k,
            stay_kernel,
            "stay",
            w_own,
            w_across,
            (*own_back, *across_back, far_back, mine, sent, tok_across),
        )
        outs.append(handed_on(layer_out))
    return jnp.concatenate(outs, axis=1)[None]


def solution(mesh):
    in_specs = (
        P("section", "expert", None),
        P("section", None),
        P("section", "expert", None),
        P("section", "expert", None),
        P("section", None, "expert"),
        P("section", None, "expert"),
        P("section", "expert", None),
    )
    out_specs = P("section", "expert", None)
    return jax.shard_map(
        on_device, mesh=mesh, in_specs=in_specs, out_specs=out_specs, check_vma=False
    )
```

```python
import functools

import jax
import jax.numpy as jnp
from jax import lax
from jax.experimental import pallas as pl
from jax.experimental.pallas import tpu as pltpu
from jax.sharding import PartitionSpec as P

EXPERTS = 4
CAP = 80
PARTS = (1792, 1792)
LAYERS = 8
TILE = 256
PACK = 128
LOAD = 46
BRING = 34
FREE = pl.CostEstimate(flops=0, bytes_accessed=0, transcendentals=0)
F32 = jnp.float32
BF16 = jnp.bfloat16
VMEM = pl.BlockSpec(memory_space=pltpu.VMEM)
ANY = pl.BlockSpec(memory_space=pl.ANY)
HBM = pl.BlockSpec(memory_space=pltpu.HBM)


def limit(mebibytes):
    return pltpu.CompilerParams(vmem_limit_bytes=mebibytes << 20)


def column():
    return lax.axis_index("expert") // 4


def swapped():
    return lax.axis_index("section") % LAYERS == LAYERS - 1


def moved(value, dx, dy, dc):
    pairs = []
    for i in range(16):
        x, y, c = i // 4, (i // 2) % 2, i % 2
        pairs.append((i, ((x + dx) % 4) * 4 + ((y + dy) % 2) * 2 + (c + dc) % 2))
    return lax.ppermute(value, "expert", pairs)


def handed_on(value):
    pairs = []
    for s in range(16):
        for e in range(16):
            to = e ^ 2 if s % LAYERS == LAYERS - 1 else e
            pairs.append((s * 16 + e, ((s + 1) % 16) * 16 + to))
    return lax.ppermute(value, ("section", "expert"), pairs)


def first_route_kernel(*refs):
    far, refs = refs[:4], refs[4:]
    *refs, sent_ref, gain_ref, ids_ref, gv_ref, sems = refs
    count, dim = far[0].shape
    near = (sent_ref.at[:, :dim], gain_ref, ids_ref, gv_ref)
    copies = [pltpu.make_async_copy(a, b, sems.at[i]) for i, (a, b) in enumerate(zip(far, near))]
    for copy in copies:
        copy.start()
    for copy in copies:
        copy.wait()
    ids, gv = ids_ref[...], gv_ref[...]
    high = gv.astype(BF16).astype(F32)
    middle = (gv - high).astype(BF16).astype(F32)
    low = gv - high - middle
    packed = jnp.concatenate([ids.astype(F32), high, middle, low], axis=0)
    packed = jnp.concatenate([packed, jnp.zeros((PACK - 8, count), F32)], axis=0)
    sent_ref[:, dim:] = packed.T.astype(BF16)
    route_kernel((0, 1, 2, 3), sent_ref, gain_ref, ids, gv, *refs)


def second_route_kernel(sent_ref, gain_ref, *refs):
    packed = sent_ref[:, gain_ref.shape[1] :].astype(F32).T
    ids = packed[0:2].astype(jnp.int32)
    gv = packed[2:4] + packed[4:6] + packed[6:8]
    route_kernel((0, 1, 3), sent_ref, gain_ref, ids, gv, *refs)


def route_kernel(kinds, tok_ref, gain_ref, ids, gv, *refs):
    w_ref = refs[-1]
    out_refs = dict(zip(kinds, refs[-1 - len(kinds) : -1]))
    wide = tok_ref[:, : gain_ref.shape[1]].astype(F32)
    scale = lax.rsqrt(jnp.mean(wide * wide, axis=-1, keepdims=True) + 1e-06)
    normed = (wide * scale * gain_ref[...]).astype(BF16)
    count = normed.shape[0]
    ids = jnp.bitwise_and(ids + (EXPERTS - column()), EXPERTS - 1)
    first, second = ids[0:1, :], ids[1:2, :]
    kind = lax.broadcasted_iota(jnp.int32, (16, count), 0)
    chosen = (kind == first) | (kind == second)
    before = (
        lax.broadcasted_iota(jnp.int32, (count, count), 0)
        < lax.broadcasted_iota(jnp.int32, (count, count), 1)
    )
    place = jnp.dot(
        chosen.astype(F32).astype(BF16), before.astype(F32).astype(BF16), preferred_element_type=F32
    )
    weight = jnp.where(kind == first, gv[0:1, :], 0.0) + jnp.where(
        kind == second, gv[1:2, :], 0.0
    )
    slot = lax.broadcasted_iota(jnp.int32, (CAP, count), 0).astype(F32)
    for d in range(EXPERTS):
        spot = jnp.where(chosen[d : d + 1, :], place[d : d + 1, :], -1.0)
        hit = slot == spot
        pick = jnp.where(hit, 1.0, 0.0).astype(BF16)
        if d in out_refs:
            out_refs[d][...] = jnp.dot(pick, normed, preferred_element_type=F32).astype(BF16)
        full = jnp.where(hit, weight[d : d + 1, :], 0.0)
        high = full.astype(BF16)
        low = (full - high.astype(F32)).astype(BF16)
        w_ref[d] = jnp.concatenate([high, low], axis=1)


def route(first_set, tok, gain, choices, others):
    count, dim = tok.shape[0], gain.shape[1]
    blocks = 4 if first_set else 3
    out_shape = [jax.ShapeDtypeStruct((CAP, dim), BF16)] * blocks
    out_shape.append(jax.ShapeDtypeStruct((EXPERTS, CAP, 2 * count), BF16))
    kernel, scratch = second_route_kernel, []
    if first_set:
        kernel = first_route_kernel
        out_shape.append(jax.ShapeDtypeStruct((count, dim + PACK), BF16))
        scratch = [pltpu.VMEM(v.shape, v.dtype) for v in (gain, *choices)]
        scratch.append(pltpu.SemaphoreType.DMA((4,)))
    operands = (tok, gain, *choices)
    inner = len(operands)

    def body(*refs):
        kernel(*refs[:inner], *refs[inner + len(others) :])

    return pl.pallas_call(
        body,
        out_shape=out_shape,
        in_specs=[HBM if first_set else VMEM] * len(operands) + [ANY] * len(others),
        out_specs=[VMEM] * len(out_shape),
        scratch_shapes=scratch,
        cost_estimate=FREE,
        compiler_params=limit(58 if first_set else 12),
        name="route",
    )(*operands, *others)


def hidden_tile(rows_ref, gate_ref, up_ref, hidden_ref, at, to):
    columns = pl.ds(at, TILE)
    gate = jnp.dot(rows_ref[...], gate_ref[:, columns], preferred_element_type=F32)
    upward = jnp.dot(rows_ref[...], up_ref[:, columns], preferred_element_type=F32)
    hidden_ref[:, pl.ds(to, TILE)] = (jax.nn.silu(gate) * upward).astype(BF16)


def load_kernel(count, *refs):
    sems = refs[-1]
    copies = [
        pltpu.make_async_copy(refs[i], refs[i - 1 - count], sems.at[i]) for i in range(count)
    ]
    for copy in copies:
        copy.start()
    for copy in copies:
        copy.wait()


def load(weights, others, room):
    count = len(weights)
    return pl.pallas_call(
        functools.partial(load_kernel, count),
        out_shape=[jax.ShapeDtypeStruct(w.shape, BF16) for w in weights],
        in_specs=[HBM] * count + [ANY] * len(others),
        out_specs=[VMEM] * count,
        scratch_shapes=[pltpu.SemaphoreType.DMA((count,))],
        cost_estimate=FREE,
        compiler_params=limit(room),
        name="load",
    )(*weights, *others)


def expert_kernel(splits, far, *refs):
    blocks = len(splits)
    rows_in, weights, refs = refs[:blocks], refs[blocks : blocks + 6], refs[blocks + 6 :]
    far_refs, refs = refs[:far], refs[far:]
    *outs, rows_ref, hidden_ref = refs
    dim, units = weights[0].shape
    for i, ref in enumerate(rows_in):
        rows_ref[i * CAP : (i + 1) * CAP, :] = ref[...]
    for half in range(2):
        for at in range(0, units, TILE):
            hidden_tile(
                rows_ref, weights[3 * half], weights[3 * half + 1], hidden_ref, at, half * units + at
            )
    for at in range(0, dim, TILE):
        columns = slice(at, at + TILE)
        total = jnp.dot(
            hidden_ref[:, :units], weights[2][:, columns], preferred_element_type=F32
        ) + jnp.dot(hidden_ref[:, units:], weights[5][:, columns], preferred_element_type=F32)
        first = 0
        for i, split in enumerate(splits):
            part = total[i * CAP : (i + 1) * CAP].astype(BF16)
            chunk = sum(1 for k in range(len(split)) if at >= sum(split[: k + 1]))
            to = at - sum(split[:chunk])
            outs[first + chunk][:, to : to + TILE] = part
            first += len(split)
    if far:
        far_ref, cross_ref, kept_ref = far_refs[0], outs[0], outs[-1]

        @pl.when(jnp.logical_not(swapped()))
        def _():
            kept_ref[...] = far_ref[...]

        @pl.when(swapped())
        def _():
            kept_ref[...] = cross_ref[...]
            cross_ref[...] = far_ref[...]


def expert(rows, weights, splits, far=(), others=()):
    blocks, dim = len(rows), rows[0].shape[1]
    units = weights[0].shape[1]
    inner = blocks + 6 + len(far)
    out_shape = [
        jax.ShapeDtypeStruct((CAP, width), BF16) for split in splits for width in split
    ] + [jax.ShapeDtypeStruct((CAP, dim), BF16)] * len(far)
    scratch = [
        pltpu.VMEM((blocks * CAP, dim), BF16),
        pltpu.VMEM((blocks * CAP, 2 * units), BF16),
    ]

    def body(*refs):
        expert_kernel(splits, len(far), *refs[:inner], *refs[inner + len(others) :])

    outs = pl.pallas_call(
        body,
        out_shape=out_shape,
        in_specs=[VMEM] * inner
        + [ANY] * len(others),
        out_specs=[VMEM] * len(out_shape),
        scratch_shapes=scratch,
        cost_estimate=FREE,
        compiler_params=limit(10),
        name="expert",
    )(*rows, *weights, *far, *others)
    grouped, first = [], 0
    for split in splits:
        group = outs[first : first + len(split)]
        grouped.append(group if len(split) > 1 else group[0])
        first += len(split)
    return grouped, list(outs[first:])


def add_kernel(a_ref, b_ref, *out_refs):
    at = 0
    for ref in out_refs:
        columns = slice(at, at + ref.shape[1])
        ref[...] = (a_ref[:, columns].astype(F32) + b_ref[:, columns].astype(F32)).astype(BF16)
        at += ref.shape[1]


def added(a, b):
    return pl.pallas_call(
        add_kernel,
        out_shape=[jax.ShapeDtypeStruct((a.shape[0], width), a.dtype) for width in PARTS],
        in_specs=[VMEM] * 2,
        out_specs=[VMEM] * len(PARTS),
        cost_estimate=FREE,
        compiler_params=limit(2),
        name="add",
    )(a, b)


def join_kernel(a_ref, b_ref, out_ref, sems):
    width = a_ref.shape[1]
    copies = [
        pltpu.make_async_copy(a_ref, out_ref.at[:, :width], sems.at[0]),
        pltpu.make_async_copy(b_ref, out_ref.at[:, width:], sems.at[1]),
    ]
    for copy in copies:
        copy.start()
    for copy in copies:
        copy.wait()


def joined(parts):
    return pl.pallas_call(
        join_kernel,
        out_shape=jax.ShapeDtypeStruct((parts[0].shape[0], sum(PARTS)), BF16),
        in_specs=[VMEM] * 2,
        out_specs=HBM,
        scratch_shapes=[pltpu.SemaphoreType.DMA((2,))],
        cost_estimate=FREE,
        compiler_params=limit(2),
        name="join",
    )(*parts)


def after_kernel(*refs):
    pass


def after(values, others):
    return pl.pallas_call(
        after_kernel,
        out_shape=[jax.ShapeDtypeStruct(v.shape, v.dtype) for v in values],
        in_specs=[ANY] * (len(values) + len(others)),
        out_specs=[ANY] * len(values),
        input_output_aliases={i: i for i in range(len(values))},
        cost_estimate=FREE,
        compiler_params=limit(1),
        name="after",
    )(*values, *others)


def weighted(w_ref, kinds, refs, columns):
    count = w_ref.shape[2] // 2
    weights = jnp.concatenate([w_ref[d] for d in kinds], axis=0)
    width = columns.stop - columns.start
    rows = jnp.concatenate(
        [ref[...] if ref.shape[1] == width else ref[:, columns] for ref in refs], axis=0
    )
    both = lax.dot_general(weights, rows, (((0,), (0,)), ((), ())), preferred_element_type=F32)
    return both[:count] + both[count:]


def leave_kernel(columns, w_own_ref, w_across_ref, *refs):
    own_refs, across_refs, out_ref = refs[:3], refs[3:6], refs[6]

    @pl.when(jnp.logical_not(swapped()))
    def _():
        out_ref[...] = weighted(w_across_ref, (0, 1, 3), across_refs, columns).astype(BF16)

    @pl.when(swapped())
    def _():
        out_ref[...] = weighted(w_own_ref, (0, 1, 3), own_refs, columns).astype(BF16)


def stay_kernel(columns, w_own_ref, w_across_ref, *refs):
    own_refs, across_refs = refs[:3], refs[3:6]
    far_ref, mine_ref, tok_ref, tok_across_ref, out_ref = refs[6:]

    def finish(w_ref, near, home_ref):
        total = weighted(w_ref, (0, 1, 3, 2), (*near, far_ref), columns)
        total += mine_ref[...].astype(F32) + home_ref[:, columns].astype(F32)
        out_ref[...] = total.astype(BF16)

    @pl.when(jnp.logical_not(swapped()))
    def _():
        finish(w_own_ref, own_refs, tok_ref)

    @pl.when(swapped())
    def _():
        finish(w_across_ref, across_refs, tok_across_ref)


def mix(chunk, kernel, name, w_own, w_across, blocks):
    count, width = w_own.shape[2] // 2, PARTS[chunk]
    begin = sum(PARTS[:chunk])
    return pl.pallas_call(
        functools.partial(kernel, slice(begin, begin + width)),
        out_shape=jax.ShapeDtypeStruct((count, width), BF16),
        in_specs=[VMEM] * (2 + len(blocks)),
        out_specs=VMEM,
        cost_estimate=FREE,
        compiler_params=limit(8),
        name=name,
    )(w_own, w_across, *blocks)


def on_device(tokens, norm_gain, expert_ids, gate_values, gate_weight, up_weight, down_weight):
    tok = tokens[0]
    dim = tok.shape[1]
    ids = expert_ids[0].T
    gv = gate_values[0].T
    gates = (gate_weight[0], moved(gate_weight[0], 0, 0, 1))
    ups = (up_weight[0], moved(up_weight[0], 0, 0, 1))
    downs = (down_weight[0], moved(down_weight[0], 0, 0, 1))

    *own, w_own, sent = route(True, tok, norm_gain, (ids, gv), ())
    tok_across = moved(sent, 0, 1, 0)
    own_far = moved(own[2], 2, 0, 0)
    held = load((gates[0], ups[0], downs[0]), (sent,), LOAD)
    right_rows, left_rows = after((own[1], own[3]), (gates[1], ups[1], downs[1], held[0]))
    own_right = moved(right_rows, 1, 0, 0)
    own_left = moved(left_rows, -1, 0, 0)
    held_more = load((gates[1], ups[1], downs[1]), (own_far,), BRING)
    (own_far,) = after((own_far,), (right_rows, left_rows, tok_across))
    across_far = moved(own_far, 0, 1, 0)
    kept = (*held, *held_more)
    whole, split = (dim,), PARTS
    *across, w_across = route(False, tok_across, norm_gain, (), (kept[3],))
    (own_out, far_out, right_out, left_out), _ = expert(
        (own[0], own_far, own_right, own_left), kept, (whole,) * 4
    )
    across_right = moved(across[1], 1, 0, 0)
    across_left = moved(across[2], -1, 0, 0)
    (far_cross, across_out), (far_kept,) = expert(
        (across_far, across[0]), kept, (whole,) * 2, (far_out,)
    )
    (right_late, left_late), _ = expert(
        (across_right, across_left), kept, (split,) * 2, others=(far_cross,)
    )
    my_right = moved(right_out, -1, 0, 0)
    my_left = moved(left_out, 1, 0, 0)
    far_in = moved(far_cross, 0, 1, 0)
    sums = added(far_kept, far_in)
    outs = []
    for k in range(len(PARTS)):
        right_rows, left_rows = right_late[k], left_late[k]
        if k > 0:
            right_rows, left_rows = after((right_rows, left_rows), (my_right, my_left))
        own_back = (own_out, my_right, my_left)
        across_back = (across_out, moved(right_rows, -1, 0, 0), moved(left_rows, 1, 0, 0))
        far_rows = sums[k]
        if k > 0:
            (far_rows,) = after((far_rows,), (arrived,))
        far_back = moved(far_rows, 2, 0, 0)
        leaving = mix(k, leave_kernel, "leave", w_own, w_across, (*own_back, *across_back))
        mine, arrived = moved(leaving, 0, 1, 0), far_back
        layer_out = mix(
            k,
            stay_kernel,
            "stay",
            w_own,
            w_across,
            (*own_back, *across_back, far_back, mine, sent, tok_across),
        )
        outs.append(handed_on(layer_out))
    return joined(outs)[None]


def solution(mesh):
    in_specs = (
        P("section", "expert", None),
        P("section", None),
        P("section", "expert", None),
        P("section", "expert", None),
        P("section", None, "expert"),
        P("section", None, "expert"),
        P("section", "expert", None),
    )
    out_specs = P("section", "expert", None)
    return jax.shard_map(
        on_device, mesh=mesh, in_specs=in_specs, out_specs=out_specs, check_vma=False
    )
```
